32 devices in a mesh: fsdp: 32 (over z, y, x, core).
Axes of the slice: x: 2, y: 2, z: 4, core: 2. Of those that a mesh axis runs over, the one named last changes fastest.
Arguments:
- tokens: bfloat16 [128, 196, 768], P('fsdp'), may hold values from -6 to 6
- cotangent: bfloat16 [128, 196, 768], P('fsdp'), may hold values from -6 to 6
- lengths: int32 [128], P('fsdp'), may hold values from 144 to 196, as said below
- ln1_gain: bfloat16 [768], P('fsdp'), may hold values from 0.5 to 1.5
- ln1_bias: bfloat16 [768], P('fsdp'), may hold values from -3 to 3
- qkv_weight: bfloat16 [768, 2304], P(None, 'fsdp'), may hold values from -0.21875 to 0.21875
- q_bias: bfloat16 [768], P('fsdp'), may hold values from -3 to 3
- v_bias: bfloat16 [768], P('fsdp'), may hold values from -3 to 3
- out_weight: bfloat16 [768, 768], P(None, 'fsdp'), may hold values from -0.625 to 0.625
- out_bias: bfloat16 [768], P('fsdp'), may hold values from -3 to 3
- ln2_gain: bfloat16 [768], P('fsdp'), may hold values from 0.5 to 1.5
- ln2_bias: bfloat16 [768], P('fsdp'), may hold values from -3 to 3
- up_weight: bfloat16 [768, 3072], P(None, 'fsdp'), may hold values from -0.21875 to 0.21875
- up_bias: bfloat16 [3072], P('fsdp'), may hold values from -3 to 3
- down_weight: bfloat16 [3072, 768], P(None, 'fsdp'), may hold values from -0.109375 to 0.109375
- down_bias: bfloat16 [768], P('fsdp'), may hold values from -3 to 3
Outputs:
- output: bfloat16 [128, 196, 768], P('fsdp')
- input_grad: float32 [128, 196, 768], P('fsdp')
- ln1_gain_grad: float32 [768], P('fsdp')
- ln1_bias_grad: float32 [768], P('fsdp')
- qkv_weight_grad: float32 [768, 2304], P(None, 'fsdp')
- q_bias_grad: float32 [768], P('fsdp')
- v_bias_grad: float32 [768], P('fsdp')
- out_weight_grad: float32 [768, 768], P(None, 'fsdp')
- out_bias_grad: float32 [768], P('fsdp')
- ln2_gain_grad: float32 [768], P('fsdp')
- ln2_bias_grad: float32 [768], P('fsdp')
- up_weight_grad: float32 [768, 3072], P(None, 'fsdp')
- up_bias_grad: float32 [3072], P('fsdp')
- down_weight_grad: float32 [3072, 768], P(None, 'fsdp')
- down_bias_grad: float32 [768], P('fsdp')
The draws below stay inside these ranges and needn't reach their ends.
Inputs may be any that keep to these rules, and one draw needn't show every extreme that they name: `lengths`: each image has 144 or 196 patches; some image has 196.
All inputs are finite; a program needn't handle non-finite values.
Results may differ from the reference program's by a relative error of at most 0.012.
Values may be sent and summed in bfloat16 or wider, within the bound.
No kernel may reach another device: no remote copies, remote signals or barrier semaphores. Data moves between devices by JAX's collectives and lax.ppermute only.
A program may use at most 192 MiB of HBM per device.

```python
import math
import jax
import jax.numpy as jnp
from jax import lax

D = 768
H = 12
HD = 64
FF = 3072
SLOTS = 196
SHORT = 144
IMAGES = 128


def draw_lengths(key, part):
    key = jax.random.fold_in(key, 7)
    picks = jax.random.randint(key, (IMAGES,), 0, 2)
    counts = SHORT + (SLOTS - SHORT) * picks
    return counts.at[0].set(SLOTS).astype(jnp.int32)


def strengthened(values, own_key, source, target, blocks, factor):
    def block_of(position):
        return (jnp.arange(values.shape[position]) // (values.shape[position] // blocks)).reshape((-1,) + (1,) * (values.ndim - 1 - position))

    near = jax.random.permutation(own_key, blocks)[block_of(target)]
    far = (block_of(target) + blocks // 2) % blocks
    return jnp.where((block_of(source) == near) | (block_of(source) == far), factor * values, values)


def block_scale(key, shape, shards, smallest, largest):
    def one(position, shards_of):
        steps = jax.random.uniform(jax.random.fold_in(jax.random.fold_in(key, 6), position), (shards_of,), jnp.float32, smallest / len(shards), largest / len(shards))
        return jnp.repeat(jnp.exp(steps), shape[position] // shards_of).reshape((-1,) + (1,) * (len(shape) - position - 1))

    gain = one(*shards[0])
    for cut in shards[1:]:
        gain = gain * one(*cut)
    return gain


def scatter_about(rng, extent, spread, reach, split=(), held_as=jnp.bfloat16):
    gain = block_scale(rng, extent, split, -0.22, 0.18) if split else 1.0
    entries = jax.random.normal(rng, extent, jnp.float32) * spread * gain
    return jnp.minimum(jnp.maximum(entries, -reach), reach).astype(held_as)


def gaussian_with(key, shape, width, most, shards, heavy, kind=jnp.bfloat16):
    drawn = width * jax.random.normal(key, shape, jnp.float32)
    if shards:
        drawn = drawn * block_scale(key, shape, shards, -0.22, 0.18)
    return jnp.clip(strengthened(drawn, jax.random.fold_in(key, 3), *heavy), -most, most).astype(kind)


def setup_inputs(seed: int = 0) -> dict:
    splits = jax.random.split(jax.random.key(seed), 17)
    return {
        "tokens": scatter_about(splits[0], (IMAGES, SLOTS, D), 1.0, 6.0, ((0, 32),)),
        "cotangent": gaussian_with(splits[1], (IMAGES, SLOTS, D), 1.0, 6.0, ((0, 32),), (0, 2, 32, 2.75)),
        "lengths": draw_lengths(jax.random.fold_in(splits[16], 71), 0),
        "ln1_gain": jnp.clip(1.0 + 0.1 * jax.random.normal(splits[3], (D,), jnp.float32), 0.5, 1.5).astype(jnp.bfloat16),
        "ln1_bias": scatter_about(splits[4], (D,), 0.3, 3.0, ((0, 32),)),
        "qkv_weight": scatter_about(splits[5], (D, 3 * D), D ** -0.5, 0.21875, ((1, 32),)),
        "q_bias": scatter_about(splits[6], (D,), 0.5, 3.0, ((0, 32),)),
        "v_bias": scatter_about(splits[7], (D,), 0.5, 3.0, ((0, 32),)),
        "out_weight": scatter_about(splits[8], (D, D), (D // 8) ** -0.5, 0.625, ((1, 32),)),
        "out_bias": scatter_about(splits[9], (D,), 0.5, 3.0, ((0, 32),)),
        "ln2_gain": jnp.clip(1.0 + 0.1 * jax.random.normal(splits[10], (D,), jnp.float32), 0.5, 1.5).astype(jnp.bfloat16),
        "ln2_bias": scatter_about(splits[11], (D,), 0.3, 3.0, ((0, 32),)),
        "up_weight": scatter_about(splits[12], (D, FF), D ** -0.5, 0.21875, ((1, 32),)),
        "up_bias": scatter_about(splits[13], (FF,), 0.5, 3.0, ((0, 32),)),
        "down_weight": scatter_about(splits[14], (FF, D), FF ** -0.5, 0.109375, ((1, 32),)),
        "down_bias": scatter_about(splits[15], (D,), 0.5, 3.0, ((0, 32),)),
    }


epsilon = 1e-06

@jax.custom_vjp
def low(v):
    return lax.optimization_barrier(v.astype(jnp.bfloat16)).astype(jnp.float32)

@jax.custom_vjp
def low_back(v):
    return v

def low_keep(v):
    return (low(v), None)

def low_pass(kept, grad):
    return (grad,)

def back_keep(v):
    return (v, None)

def back_low(kept, grad):
    return (low(grad),)
low.defvjp(low_keep, low_pass)
low_back.defvjp(back_keep, back_low)

def normalize(values):
    center = values - lax.optimization_barrier(jnp.mean(values, axis=-1, keepdims=True))
    return center * lax.rsqrt(lax.optimization_barrier(jnp.mean(center * center, axis=-1, keepdims=True)) + epsilon)

def forward(tokens, lengths, ln1_gain, ln1_bias, qkv_weight, q_bias, v_bias, out_weight, out_bias, ln2_gain, ln2_bias, up_weight, up_bias, down_weight, down_bias):
    highest = lax.Precision.HIGHEST
    image_count = tokens.shape[0]
    normed_low = low(normalize(tokens) * ln1_gain + ln1_bias)
    qkv_bias = jnp.concatenate([q_bias, jnp.zeros_like(q_bias), v_bias])
    qkv_rows = jnp.einsum('gsd,de->gse', normed_low, qkv_weight, precision=highest) + qkv_bias
    qkv_rows = low_back(low(qkv_rows)).reshape(image_count, SLOTS, 3, H, HD)
    query_rows = qkv_rows[:, :, 0]
    key_rows = qkv_rows[:, :, 1]
    value_rows = qkv_rows[:, :, 2]
    scores = jnp.einsum('gqhe,gkhe->ghqk', query_rows, key_rows, precision=highest) * HD ** (-0.5)
    scores = low_back(scores)
    key_live = jnp.arange(SLOTS, dtype=jnp.int32)[None, :] < lengths[:, None]
    scores = jnp.where(key_live[:, None, None, :], scores, -1e+30)
    attend = low(jax.nn.softmax(scores, axis=-1))
    mixture = jnp.einsum('ghqk,gkhe->gqhe', attend, value_rows, precision=highest).reshape(image_count, SLOTS, D)
    mixture = low_back(low(mixture))
    branch = jnp.einsum('gsd,de->gse', mixture, out_weight, precision=highest) + out_bias
    middle = tokens + low_back(branch)
    normed_two = low(normalize(middle) * ln2_gain + ln2_bias)
    pre_gelu = low_back(jnp.einsum('gsd,df->gsf', normed_two, up_weight, precision=highest) + up_bias)
    hidden = low(jax.nn.gelu(pre_gelu, approximate=False))
    feed = jnp.einsum('gsf,fd->gsd', hidden, down_weight, precision=highest) + down_bias
    return middle + low_back(feed)

def reference(tokens, cotangent, lengths, ln1_gain, ln1_bias, qkv_weight, q_bias, v_bias, out_weight, out_bias, ln2_gain, ln2_bias, up_weight, up_bias, down_weight, down_bias):
    params = tuple((member.astype(jnp.float32) for member in (ln1_gain, ln1_bias, qkv_weight, q_bias, v_bias, out_weight, out_bias, ln2_gain, ln2_bias, up_weight, up_bias, down_weight, down_bias)))
    group_size = math.gcd(IMAGES, 16)
    group_count = IMAGES // group_size
    blocks = tokens.astype(jnp.float32).reshape(group_count, group_size, SLOTS, D)
    cot_blocks = cotangent.astype(jnp.float32).reshape(group_count, group_size, SLOTS, D)
    length_blocks = lengths.reshape(group_count, group_size)

    def group_step(totals, pieces):
        inputs_block, cot_block, block_lengths = pieces

        def apply_layer(inputs, *weights):
            return forward(inputs, block_lengths, *weights)
        result, pullback = jax.vjp(apply_layer, inputs_block, *params)
        gradients = pullback(cot_block)
        summed = tuple((running + update for running, update in zip(totals, gradients[1:])))
        return (summed, (result.astype(jnp.bfloat16), gradients[0]))
    initial = tuple((jnp.zeros_like(member) for member in params))
    totals, (results, input_grads) = lax.scan(group_step, initial, (blocks, cot_blocks, length_blocks))
    output = results.reshape(IMAGES, SLOTS, D)
    input_grad = input_grads.reshape(IMAGES, SLOTS, D)
    return (output, input_grad, totals[0], totals[1], totals[2], totals[3], totals[4], totals[5], totals[6], totals[7], totals[8], totals[9], totals[10], totals[11], totals[12])
```

```python
import functools

import jax
import jax.numpy as jnp
from jax import lax
from jax.experimental import pallas as pl
from jax.experimental.pallas import tpu as pltpu
from jax.sharding import PartitionSpec as P

H = 12
HD = 64
EPS = 1e-06
BF = jnp.bfloat16
F32 = jnp.float32
VMEM_LIMIT = 56 * 1024 * 1024
CHUNKS = 2


def dot(left, right, left_dim, right_dim):
    return lax.dot_general(
        left, right, (((left_dim,), (right_dim,)), ((), ())), preferred_element_type=F32
    )


def norm_parts(values):
    center = values - jnp.mean(values, axis=-1, keepdims=True)
    rscale = lax.rsqrt(jnp.mean(center * center, axis=-1, keepdims=True) + EPS)
    return center * rscale, rscale


def norm_back(grad_normal, normal, rscale):
    grad_mean = jnp.mean(grad_normal, axis=-1, keepdims=True)
    grad_cross = jnp.mean(grad_normal * normal, axis=-1, keepdims=True)
    return rscale * (grad_normal - grad_mean - normal * grad_cross)


def gelu_parts(values):
    size = jnp.abs(values)
    step = 1.0 / (1.0 + (0.3275911 * 0.7071067811865476) * size)
    bell = jnp.exp(-0.5 * values * values)
    poly = 1.061405429 * 0.5
    for factor in (-1.453152027, 1.421413741, -0.284496736, 0.254829592):
        poly = poly * step + 0.5 * factor
    tail = poly * step * bell
    return jnp.where(values >= 0, 1.0 - tail, tail), values * bell * 0.3989422804014327


def params(**more):
    return pltpu.CompilerParams(vmem_limit_bytes=VMEM_LIMIT, **more)


def cost(flops, moved):
    return pl.CostEstimate(flops=flops, bytes_accessed=moved, transcendentals=0)


def qkv_body(tokens, vectors, bias, weight, normed, qkv):
    @pl.when(pl.program_id(0) == 0)
    def first():
        rows = normed.shape[0] // 13

        def block(index, carry):
            at = pl.ds(pl.multiple_of(index * rows, rows), rows)
            normal, _ = norm_parts(tokens[at, :].astype(F32))
            normed[at, :] = (normal * vectors[0:1, :] + vectors[1:2, :]).astype(BF)
            return carry

        lax.fori_loop(0, 13, block, 0)

    qkv[...] = (dot(normed[...], weight[...], 1, 1) + bias[...]).astype(BF)


def qkv_call(tokens, vectors, bias, weight):
    rows, width = tokens.shape
    return pl.pallas_call(
        qkv_body,
        grid=(3,),
        in_specs=[
            pl.BlockSpec((rows, width), lambda j: (0, 0)),
            pl.BlockSpec((8, width), lambda j: (0, 0)),
            pl.BlockSpec((1, width), lambda j: (0, j)),
            pl.BlockSpec((width, width), lambda j: (j, 0)),
        ],
        out_specs=[
            pl.BlockSpec((rows, width), lambda j: (0, 0)),
            pl.BlockSpec((rows, width), lambda j: (0, j)),
        ],
        out_shape=[
            jax.ShapeDtypeStruct((rows, width), BF),
            jax.ShapeDtypeStruct((rows, 3 * width), BF),
        ],
        compiler_params=params(),
        cost_estimate=cost(6 * rows * width * width, 2 * (5 * rows * width + 3 * width * width)),
        name="qkv",
    )(tokens, vectors, bias, weight)


def attend_body(lengths, qkv, tokens, vectors, weight, mixture, middle, normed):
    slots, width = tokens.shape
    live = lax.broadcasted_iota(jnp.int32, (slots, slots), 1) < lengths[pl.program_id(0)]
    near = lax.broadcasted_iota(jnp.int32, (slots, 2 * HD), 1) < HD
    for pair in range(H // 2):
        at = 2 * HD * pair
        query = qkv[:, at : at + 2 * HD] * HD**-0.5
        key = qkv[:, width + at : width + at + 2 * HD]
        value = qkv[:, 2 * width + at : 2 * width + at + 2 * HD]
        mixed = []
        for half in (near, ~near):
            scores = dot(jnp.where(half, query, 0), key, 1, 1)
            scores = jnp.where(live, scores, -1e30)
            powers = jnp.exp(scores - jnp.max(scores, axis=1, keepdims=True))
            weights = powers * (1.0 / jnp.sum(powers, axis=1, keepdims=True))
            mixed.append(dot(weights.astype(BF), value, 1, 0))
        mixture[:, at : at + 2 * HD] = jnp.where(near, mixed[0], mixed[1]).astype(BF)
    branch = dot(mixture[...], weight[...], 1, 1)
    middle[...] = branch + (tokens[...].astype(F32) + vectors[4:5, :])
    normal, _ = norm_parts(middle[...])
    normed[...] = (normal * vectors[5:6, :] + vectors[6:7, :]).astype(BF)


def attend_call(lengths, qkv, tokens, vectors, weight):
    rows, width = tokens.shape
    images = lengths.shape[0]
    slots = rows // images
    row = pl.BlockSpec((slots, width), lambda i, *_: (i, 0))
    return pl.pallas_call(
        attend_body,
        grid_spec=pltpu.PrefetchScalarGridSpec(
            num_scalar_prefetch=1,
            grid=(images,),
            in_specs=[
                pl.BlockSpec((slots, 3 * width), lambda i, *_: (i, 0)),
                row,
                pl.BlockSpec((8, width), lambda i, *_: (0, 0)),
                pl.BlockSpec((width, width), lambda i, *_: (0, 0)),
            ],
            out_specs=[row, row, row],
        ),
        out_shape=[
            jax.ShapeDtypeStruct((rows, width), BF),
            jax.ShapeDtypeStruct((rows, width), F32),
            jax.ShapeDtypeStruct((rows, width), BF),
        ],
        compiler_params=params(),
        cost_estimate=cost(16 * rows * width * width, 16 * rows * width),
        name="attend",
    )(lengths, qkv, tokens, vectors, weight)


def feed_body(hops, *refs):
    if hops:
        table, normed, cot, up, down, bias, feed, back, bias_grad = refs[:9]
        groups, hidden, slope, held = refs[9:13], refs[13], refs[14], refs[15]
    else:
        normed, cot, up, down, bias, feed, back, bias_grad, up_grad, down_grad, hidden, slope = refs
    step = pl.program_id(0)
    slots = normed.shape[0] // 4
    total = jnp.zeros_like(bias_grad)
    for part in range(4):
        at = slice(slots * part, slots * (part + 1))
        before = dot(normed[at, :], up[...], 1, 1) + bias[...]
        grad = dot(cot[at, :], down[...], 1, 0)
        share, bend = gelu_parts(before)
        hidden[at, :] = (before * share).astype(BF)
        low = (grad * (share + bend)).astype(BF)
        slope[at, :] = low
        total += jnp.sum(low.astype(F32), axis=0, keepdims=True)
        ahead = dot(hidden[at, :], down[...], 1, 1)
        behind = dot(low, up[...], 1, 0)

        @pl.when(step == 0)
        def start():
            feed[at, :] = ahead
            back[at, :] = behind

        @pl.when(step != 0)
        def go():
            feed[at, :] += ahead
            back[at, :] += behind

    bias_grad[...] = total
    up_found = dot(slope[...], normed[...], 0, 0)
    down_found = dot(cot[...], hidden[...], 0, 0)
    if not hops:
        up_grad[...] = up_found.astype(BF)
        down_grad[...] = down_found.astype(BF)
        return
    width = normed.shape[1]
    tiles = held.shape[1] * 256 // (2 * width)
    many = width // (32 // tiles)
    for owner in range(32 // tiles):
        block = up_found[many * owner : many * (owner + 1)].reshape(many // 8, 8, width)
        held[step * (32 // tiles) + owner, : many // 8] = block.astype(BF)
    few = width // 32
    for owner in range(32):
        block = down_found[few * owner : few * (owner + 1)].reshape(few // 8, 8, width)
        held[owner, pl.ds(many // 8 + step * (few // 8), few // 8)] = block.astype(BF)

    @pl.when(step == tiles - 1)
    def last():
        deal(table, held, groups)


def feed_call(table, normed, cot, up, down, bias):
    hops = table is not None
    rows, width = normed.shape
    units = up.shape[0]
    whole = pl.BlockSpec((rows, width), lambda t, *_: (0, 0))
    tile = pl.BlockSpec((width, width), lambda t, *_: (t, 0))
    line = pl.BlockSpec((1, width), lambda t, *_: (0, t))
    scratch = [pltpu.VMEM((rows, width), BF), pltpu.VMEM((rows, width), BF)]
    if hops:
        block = 2 * units // 256
        more = [pl.BlockSpec((8, block, 8, width), lambda t, *_: (0, 0, 0, 0))] * 4
        shapes = group_shapes(block, width)
        scratch = scratch + [pltpu.VMEM((32, block, 8, width), BF)]
    else:
        more = [tile, tile]
        shapes = [jax.ShapeDtypeStruct((units, width), BF)] * 2
    return pl.pallas_call(
        functools.partial(feed_body, hops),
        grid_spec=pltpu.PrefetchScalarGridSpec(
            num_scalar_prefetch=1 if hops else 0,
            grid=(units // width,),
            in_specs=[whole, whole, tile, tile, line],
            out_specs=[whole, whole, line] + more,
            scratch_shapes=scratch,
        ),
        out_shape=[
            jax.ShapeDtypeStruct((rows, width), F32),
            jax.ShapeDtypeStruct((rows, width), F32),
            jax.ShapeDtypeStruct((1, units), F32),
        ]
        + shapes,
        compiler_params=params(),
        cost_estimate=cost(12 * rows * width * units, 20 * rows * width + 8 * units * width),
        name="feed",
    )(*(([table] if hops else []) + [normed, cot, up, down, bias]))


def close_body(count, *refs):
    middle, cot, vectors = refs[:3]
    feeds, backs = refs[3 : 3 + count], refs[3 + count : 3 + 2 * count]
    output, grad_middle, grad_low, sums = refs[3 + 2 * count :]
    slots = output.shape[1]
    total = feeds[0][...]
    behind = backs[0][...]
    for more in range(1, count):
        total += feeds[more][...]
        behind += backs[more][...]
    values = middle[...]
    given = cot[...].astype(F32)
    output[0] = (values + total + vectors[7:8, :])[:slots].astype(BF)
    normal, rscale = norm_parts(values)
    grad = given + norm_back(behind * vectors[5:6, :], normal, rscale)
    grad_middle[...] = grad
    low = grad.astype(BF)
    grad_low[...] = low

    @pl.when(pl.program_id(0) == 0)
    def start():
        sums[...] = jnp.zeros_like(sums)

    for place, term in enumerate((behind * normal, behind, given, low.astype(F32))):
        sums[place : place + 1, :] += jnp.sum(term, axis=0, keepdims=True)


def close_call(middle, cot, vectors, feeds, backs, images, slots):
    rows, width = middle.shape
    row = pl.BlockSpec((rows // images, width), lambda i: (i, 0))
    fixed = pl.BlockSpec((8, width), lambda i: (0, 0))
    return pl.pallas_call(
        functools.partial(close_body, len(feeds)),
        grid=(images,),
        in_specs=[row, row, fixed] + [row] * (2 * len(feeds)),
        out_specs=[pl.BlockSpec((1, slots, width), lambda i: (i, 0, 0)), row, row, fixed],
        out_shape=[
            jax.ShapeDtypeStruct((images, slots, width), BF),
            jax.ShapeDtypeStruct((rows, width), F32),
            jax.ShapeDtypeStruct((rows, width), BF),
            jax.ShapeDtypeStruct((8, width), F32),
        ],
        compiler_params=params(),
        cost_estimate=cost(50 * rows * width, 30 * rows * width),
        name="close",
    )(middle, cot, vectors, *feeds, *backs)


def attend_back_body(lengths, qkv, grad_low, weight, grad_qkv, grad_mix):
    slots, width = grad_low.shape
    live = lax.broadcasted_iota(jnp.int32, (slots, slots), 0) < lengths[pl.program_id(0)]
    near = lax.broadcasted_iota(jnp.int32, (slots, 2 * HD), 1) < HD
    grad_mix[...] = dot(grad_low[...], weight[...], 1, 0).astype(BF)
    for pair in range(H // 2):
        at = 2 * HD * pair
        query = qkv[:, at : at + 2 * HD] * HD**-0.5
        key = qkv[:, width + at : width + at + 2 * HD]
        value = qkv[:, 2 * width + at : 2 * width + at + 2 * HD]
        mix = grad_mix[:, at : at + 2 * HD]
        found = []
        for half in (near, ~near):
            scores = dot(key, jnp.where(half, query, 0), 1, 1)
            scores = jnp.where(live, scores, -1e30)
            powers = jnp.exp(scores - jnp.max(scores, axis=0, keepdims=True))
            weights = powers * (1.0 / jnp.sum(powers, axis=0, keepdims=True))
            slope = dot(value, jnp.where(half, mix, 0), 1, 1)
            grad_value = dot(weights.astype(BF), mix, 1, 0)
            inner = jnp.sum(slope * weights, axis=0, keepdims=True)
            low = (weights * (slope - inner)).astype(BF)
            grad_key = dot(low, query, 1, 0)
            grad_query = dot(low, key * HD**-0.5, 0, 0)
            found.append((grad_query, grad_key, grad_value))
        for place in range(3):
            grad_qkv[:, place * width + at : place * width + at + 2 * HD] = jnp.where(
                near, found[0][place], found[1][place]
            ).astype(BF)


def attend_back_call(lengths, qkv, grad_low, weight):
    rows, width = grad_low.shape
    images = lengths.shape[0]
    slots = rows // images
    wide = pl.BlockSpec((slots, 3 * width), lambda i, *_: (i, 0))
    return pl.pallas_call(
        attend_back_body,
        grid_spec=pltpu.PrefetchScalarGridSpec(
            num_scalar_prefetch=1,
            grid=(images,),
            in_specs=[
                wide,
                pl.BlockSpec((slots, width), lambda i, *_: (i, 0)),
                pl.BlockSpec((width, width), lambda i, *_: (0, 0)),
            ],
            out_specs=[wide],
            scratch_shapes=[pltpu.VMEM((slots, width), BF)],
        ),
        out_shape=[jax.ShapeDtypeStruct((rows, 3 * width), BF)],
        compiler_params=params(),
        cost_estimate=cost(30 * rows * width * width, 16 * rows * width),
        name="attend_back",
    )(lengths, qkv, grad_low, weight)[0]


def cross_flat_body(left, right, out):
    out[...] = dot(left[...], right[...], 0, 0).astype(BF)


def cross_flat_call(left, right):
    rows, width = right.shape
    wide = left.shape[1]
    return pl.pallas_call(
        cross_flat_body,
        grid=(wide // width,),
        in_specs=[
            pl.BlockSpec((rows, width), lambda j: (0, j)),
            pl.BlockSpec((rows, width), lambda j: (0, 0)),
        ],
        out_specs=pl.BlockSpec((width, width), lambda j: (j, 0)),
        out_shape=jax.ShapeDtypeStruct((wide, width), BF),
        compiler_params=params(),
        cost_estimate=cost(2 * rows * width * wide, 2 * rows * (width + wide) + 2 * wide * width),
        name="cross",
    )(left, right)


def deal(table, held, groups):
    for index in range(32):
        groups[index // 8][index % 8] = held[table[index]]


def group_shapes(units, width):
    return [jax.ShapeDtypeStruct((8, units, 8, width), BF)] * 4


def cross_body(table, left, right, *refs):
    groups, whole, held = refs[:4], refs[4], refs[5]
    step = pl.program_id(0)
    steps = pl.num_programs(0)
    width = right.shape[1]
    for index in range(whole.shape[0] // width):
        @pl.when(step == index)
        def tile():
            whole[width * index : width * (index + 1), :] = dot(left[...], right[...], 0, 0)

    @pl.when(step == steps - 1)
    def last():
        units = held.shape[1]
        for owner in range(32):
            block = whole[8 * units * owner : 8 * units * (owner + 1), :]
            held[owner] = block.reshape(units, 8, width).astype(BF)
        deal(table, held, groups)


def cross_call(table, left, right):
    rows, width = right.shape
    wide = left.shape[1]
    units = wide // 256
    group = pl.BlockSpec((8, units, 8, width), lambda j, *_: (0, 0, 0, 0))
    return pl.pallas_call(
        cross_body,
        grid_spec=pltpu.PrefetchScalarGridSpec(
            num_scalar_prefetch=1,
            grid=(wide // width,),
            in_specs=[
                pl.BlockSpec((rows, width), lambda j, *_: (0, j)),
                pl.BlockSpec((rows, width), lambda j, *_: (0, 0)),
            ],
            out_specs=[group] * 4,
            scratch_shapes=[pltpu.VMEM((wide, width), F32), pltpu.VMEM((32, units, 8, width), BF)],
        ),
        out_shape=group_shapes(units, width),
        compiler_params=params(),
        cost_estimate=cost(2 * rows * width * wide, 2 * rows * (width + wide) + 2 * wide * width),
        name="cross",
    )(table, left, right)


def enter_body(tokens, grad_qkv, grad_middle, vectors, weight, grad_input, sums, bias_sum):
    slots = grad_input.shape[1]
    low = grad_qkv[...]
    grad = dot(low, weight[...], 1, 0)
    normal, rscale = norm_parts(tokens[...].astype(F32))
    full = grad_middle[...] + norm_back(grad * vectors[0:1, :], normal, rscale)
    grad_input[0] = full[:slots]

    @pl.when(pl.program_id(0) == 0)
    def start():
        sums[...] = jnp.zeros_like(sums)
        bias_sum[...] = jnp.zeros_like(bias_sum)

    sums[0:1, :] += jnp.sum(grad * normal, axis=0, keepdims=True)
    sums[1:2, :] += jnp.sum(grad, axis=0, keepdims=True)
    bias_sum[...] += jnp.sum(low.astype(F32), axis=0, keepdims=True)


def enter_call(tokens, grad_qkv, grad_middle, vectors, weight, images, slots):
    rows, width = tokens.shape
    row = pl.BlockSpec((rows // images, width), lambda i: (i, 0))
    fixed = pl.BlockSpec((8, width), lambda i: (0, 0))
    return pl.pallas_call(
        enter_body,
        grid=(images,),
        in_specs=[
            row,
            pl.BlockSpec((rows // images, 3 * width), lambda i: (i, 0)),
            row,
            fixed,
            pl.BlockSpec((3 * width, width), lambda i: (0, 0)),
        ],
        out_specs=[
            pl.BlockSpec((1, slots, width), lambda i: (i, 0, 0)),
            fixed,
            pl.BlockSpec((1, 3 * width), lambda i: (0, 0)),
        ],
        out_shape=[
            jax.ShapeDtypeStruct((images, slots, width), F32),
            jax.ShapeDtypeStruct((8, width), F32),
            jax.ShapeDtypeStruct((1, 3 * width), F32),
        ],
        compiler_params=params(),
        cost_estimate=cost(6 * rows * width * width, 20 * rows * width),
        name="enter",
    )(tokens, grad_qkv, grad_middle, vectors, weight)


ORDERS = ((8, 16, 2, 4), (16, 8, 4, 2))


def reach(order):
    return [sum(order[bit] for bit in range(4) if index >> bit & 1) for index in range(16)]


def block_table():
    me = lax.axis_index("fsdp")
    near, far = reach(ORDERS[0]), reach(ORDERS[1])
    even = jnp.array(near + [1 ^ place for place in far], jnp.int32)
    odd = jnp.array(far + [1 ^ place for place in near], jnp.int32)
    return jnp.bitwise_xor(jnp.where(me % 2 == 0, even, odd), me.astype(jnp.int32))


def swap(values, step):
    pairs = [(index, index ^ (1 if step < 0 else ORDERS[index % 2][step])) for index in range(32)]
    return lax.ppermute(values, "fsdp", pairs)


def place_body(units, table, *refs):
    groups, parts = refs[:4], refs[4:]
    for index in range(32):
        owner = table[index]
        start = 0
        for part, unit in zip(parts, units):
            part[owner] = groups[index // 8][index % 8, start : start + unit]
            start += unit


def place_call(table, groups, units):
    width = groups[0].shape[-1]
    whole = pl.BlockSpec(memory_space=pltpu.VMEM)
    return pl.pallas_call(
        functools.partial(place_body, units),
        in_specs=[pl.BlockSpec(memory_space=pltpu.SMEM)] + [whole] * 4,
        out_specs=[whole] * len(units),
        out_shape=[jax.ShapeDtypeStruct((32, unit, 8, width), BF) for unit in units],
        compiler_params=params(),
        cost_estimate=cost(0, 4 * 256 * sum(units) * width),
        name="place",
    )(table, *groups)


def sort_body(units, full, *parts):
    start = 0
    for part, unit in zip(parts, units):
        part[...] = full[:, start : start + unit]
        start += unit


def sort_call(full, units):
    count, unit, _, width = full.shape
    some = 4
    return pl.pallas_call(
        functools.partial(sort_body, units),
        grid=(count // some,),
        in_specs=[pl.BlockSpec((some, unit, 8, width), lambda i: (i, 0, 0, 0))],
        out_specs=[pl.BlockSpec((some, part, 8, width), lambda i: (i, 0, 0, 0)) for part in units],
        out_shape=[jax.ShapeDtypeStruct((count, part, 8, width), BF) for part in units],
        compiler_params=params(),
        cost_estimate=cost(0, 4 * 8 * count * unit * width),
        name="sort",
    )(full)


def gather_hops(table, parts):
    width = parts[0].shape[-1]
    units = [part.shape[0] // 8 for part in parts]
    held = jnp.concatenate(parts, axis=0).reshape(1, sum(units), 8, width)
    for step in range(3):
        held = jnp.concatenate([held, swap(held, step)], axis=0)
    across = swap(held, -1)
    late = swap(held, 3)
    late_across = swap(late, -1)
    placed = place_call(table, (held, late, across, late_across), units)
    return [part.reshape(-1, width) for part in placed]


def gather_flat(count, parts):
    width = parts[0].shape[-1]
    packed = jnp.concatenate(parts, axis=0)
    full = lax.all_gather(packed, "fsdp", axis=0, tiled=True)
    if all(part.shape[0] % 8 == 0 for part in parts):
        units = [part.shape[0] // 8 for part in parts]
        full = full.reshape(count, sum(units), 8, width)
        return [part.reshape(-1, width) for part in sort_call(full, units)]
    full = full.reshape(count, -1, width)
    found = []
    start = 0
    for part in parts:
        found.append(full[:, start : start + part.shape[0]].reshape(-1, width))
        start += part.shape[0]
    return found


def scatter_hops(groups):
    near, far, near_across, far_across = groups
    far_in = swap(far_across, -1)
    near_in = swap(near_across, -1)
    moved = swap((far.astype(F32) + far_in.astype(F32)).astype(BF), 3)
    total = near.astype(F32) + near_in.astype(F32) + moved.astype(F32)
    for step in (2, 1, 0):
        half = 1 << step
        total = total[:half] + swap(total[half:].astype(BF), step).astype(F32)
    return total.reshape(-1, near.shape[-1])


def scatter_flat(parts):
    return [lax.psum_scatter(part.astype(F32), "fsdp", scatter_dimension=0, tiled=True) for part in parts]


def scatter_vector_hops(values):
    total = values
    me = lax.axis_index("fsdp")
    for bit in (0, 1, 2, 3, 4):
        count = total.shape[0] // 2
        pairs = [(index, index ^ (1 << bit)) for index in range(32)]
        split = total.reshape(count, 2, -1)
        mine = (me >> bit) & 1
        keep = jnp.where(mine == 0, split[:, 0], split[:, 1])
        send = jnp.where(mine == 0, split[:, 1], split[:, 0])
        total = keep + lax.ppermute(send, "fsdp", pairs)
    return total.reshape(-1)


def shards(
    count,
    tokens,
    cotangent,
    lengths,
    ln1_gain,
    ln1_bias,
    qkv_weight,
    q_bias,
    v_bias,
    out_weight,
    out_bias,
    ln2_gain,
    ln2_bias,
    up_weight,
    up_bias,
    down_weight,
    down_bias,
):
    images, slots, width = tokens.shape
    hops = count == 32
    padded = -(-slots // 16) * 16
    own = width // count
    units = up_bias.shape[0] // CHUNKS
    table = block_table() if hops else None

    singles = [ln1_gain, ln1_bias, q_bias, v_bias, out_bias, ln2_gain, ln2_bias, down_bias]
    vector = jnp.concatenate(singles + [up_bias])
    extra = jnp.zeros((8, width), BF).at[0, : vector.shape[0]].set(vector)
    qkv_rows = qkv_weight.T
    out_rows = out_weight.T
    up_rows = up_weight.T.reshape(CHUNKS, units, width)
    tiles = units * count // width
    down_rows = down_weight.reshape(count, CHUNKS, units, own).transpose(1, 3, 0, 2)
    down_rows = down_rows.reshape(CHUNKS, own, tiles, width).transpose(0, 2, 1, 3)

    first = [qkv_rows, extra]
    second = [out_rows] + [up_rows[chunk] for chunk in range(CHUNKS)]
    second += [down_rows[chunk, tile] for chunk in range(CHUNKS) for tile in range(tiles)]
    if hops:
        qkv_full, extra_full = gather_hops(table, first)
    else:
        qkv_full, extra_full = gather_flat(count, first)
    rest = gather_flat(count, second)
    out_full = rest[0]
    up_full = rest[1 : 1 + CHUNKS]
    down_full = [
        jnp.concatenate(rest[1 + CHUNKS + tiles * chunk : 1 + CHUNKS + tiles * (chunk + 1)])
        for chunk in range(CHUNKS)
    ]

    extra_full = extra_full.reshape(count, 8, width)[:, 0, : vector.shape[0]].astype(F32)
    vectors = extra_full[:, : 8 * own].reshape(count, 8, own).transpose(1, 0, 2).reshape(8, width)
    up_bias_full = extra_full[:, 8 * own :].reshape(count, CHUNKS, units).transpose(1, 0, 2)
    up_bias_full = up_bias_full.reshape(CHUNKS, 1, count * units)
    qkv_bias = jnp.concatenate([vectors[2], jnp.zeros((width,), F32), vectors[3]])[None]

    pad = ((0, 0), (0, padded - slots), (0, 0))
    token_rows = jnp.pad(tokens, pad).reshape(images * padded, width)
    cot_rows = jnp.pad(cotangent, pad).reshape(images * padded, width)

    normed_one, qkv = qkv_call(token_rows, vectors, qkv_bias, qkv_full)
    mixture, middle, normed_two = attend_call(lengths, qkv, token_rows, vectors, out_full)
    feeds, backs, bias_grads, sums = [], [], [], []
    for chunk in range(CHUNKS):
        feed, back, bias_grad, *found = feed_call(
            table, normed_two, cot_rows, up_full[chunk], down_full[chunk], up_bias_full[chunk]
        )
        feeds.append(feed)
        backs.append(back)
        bias_grads.append(bias_grad)
        if hops:
            sums.append(scatter_hops(found))
        else:
            split = jnp.split(found[1], tiles)
            sums.append(jnp.concatenate(scatter_flat([found[0]] + split)))
    output, grad_middle, grad_low, close_sums = close_call(
        middle, cot_rows, vectors, feeds, backs, images, slots
    )
    if hops:
        out_sum = scatter_hops(cross_call(table, grad_low, mixture))
    else:
        (out_sum,) = scatter_flat([cross_flat_call(grad_low, mixture)])
    grad_qkv = attend_back_call(lengths, qkv, grad_low, out_full)
    if hops:
        qkv_sum = scatter_hops(cross_call(table, grad_qkv, normed_one))
    else:
        (qkv_sum,) = scatter_flat([cross_flat_call(grad_qkv, normed_one)])
    grad_input, enter_sums, qkv_bias_sum = enter_call(
        token_rows, grad_qkv, grad_middle, vectors, qkv_full, images, slots
    )

    wide = qkv_bias_sum[0]
    eight = jnp.stack(
        [
            enter_sums[0],
            enter_sums[1],
            wide[:width],
            wide[2 * width :],
            close_sums[3],
            close_sums[0],
            close_sums[1],
            close_sums[2],
        ]
    )
    eight = eight.reshape(8, count, own).transpose(1, 0, 2).reshape(count, 8 * own)
    many = jnp.stack(bias_grads).reshape(CHUNKS, count, units).transpose(1, 0, 2)
    every = jnp.concatenate([eight, many.reshape(count, CHUNKS * units)], axis=1)
    if hops:
        small = scatter_vector_hops(every)
    else:
        small = lax.psum_scatter(every.reshape(-1), "fsdp", scatter_dimension=0, tiled=True)
    vec = [small[own * place : own * (place + 1)] for place in range(8)]

    up_sum = jnp.concatenate([found[:units] for found in sums]).T
    down_sum = jnp.stack([found[units:].reshape(tiles, own, width) for found in sums])
    down_sum = down_sum.transpose(0, 2, 1, 3).reshape(CHUNKS, own, count, units)
    down_sum = down_sum.transpose(2, 0, 3, 1).reshape(count * CHUNKS * units, own)
    return (
        output,
        grad_input,
        vec[0],
        vec[1],
        qkv_sum.T,
        vec[2],
        vec[3],
        out_sum.T,
        vec[4],
        vec[5],
        vec[6],
        up_sum,
        small[8 * own :],
        down_sum,
        vec[7],
    )


def solution(mesh):
    row, column, vector = P("fsdp", None, None), P(None, "fsdp"), P("fsdp")
    return jax.shard_map(
        functools.partial(shards, mesh.shape["fsdp"]),
        mesh=mesh,
        in_specs=(row, row, vector, vector, vector, column, vector, vector, column, vector)
        + (vector, vector, column, vector, column, vector),
        out_specs=(row, row, vector, vector, column, vector, vector, column, vector)
        + (vector, vector, column, vector, column, vector),
        check_vma=False,
    )
```

```python
import functools

import jax
import jax.numpy as jnp
from jax import lax
from jax.experimental import pallas as pl
from jax.experimental.pallas import tpu as pltpu
from jax.sharding import PartitionSpec as P

H = 12
HD = 64
EPS = 1e-06
BF = jnp.bfloat16
F32 = jnp.float32
MIB = 1024 * 1024
CHUNKS = 4
COST = 1
FEED_MIB = 32


def dot(left, right, left_dim, right_dim):
    return lax.dot_general(
        left, right, (((left_dim,), (right_dim,)), ((), ())), preferred_element_type=F32
    )


def norm_parts(values):
    center = values - jnp.mean(values, axis=-1, keepdims=True)
    rscale = lax.rsqrt(jnp.mean(center * center, axis=-1, keepdims=True) + EPS)
    return center * rscale, rscale


def norm_back(grad_normal, normal, rscale):
    grad_mean = jnp.mean(grad_normal, axis=-1, keepdims=True)
    grad_cross = jnp.mean(grad_normal * normal, axis=-1, keepdims=True)
    return rscale * (grad_normal - grad_mean - normal * grad_cross)


def gelu_parts(values):
    size = jnp.abs(values)
    step = 1.0 / (1.0 + (0.3275911 * 0.7071067811865476) * size)
    bell = jnp.exp(-0.5 * values * values)
    poly = 1.061405429 * 0.5
    for factor in (-1.453152027, 1.421413741, -0.284496736, 0.254829592):
        poly = poly * step + 0.5 * factor
    tail = poly * step * bell
    return jnp.where(values >= 0, 1.0 - tail, tail), values * bell * 0.3989422804014327


def params(mib=24):
    return pltpu.CompilerParams(vmem_limit_bytes=mib * MIB)


def waiting(body, inputs, spare):
    return lambda *refs: body(*refs[:inputs], *refs[inputs + spare :])


ANYWHERE = pl.BlockSpec(memory_space=pl.ANY)


def cost(flops, moved):
    return pl.CostEstimate(flops=flops // COST, bytes_accessed=moved // COST, transcendentals=0)


def still(*shape):
    return pl.BlockSpec(shape, lambda *_: (0,) * len(shape), pipeline_mode=pl.Buffered(1))


def qkv_body(tokens, vectors, weight, normed, qkv):
    step = pl.program_id(0)

    @pl.when(step == 0)
    def first():
        rows = normed.shape[0] // 13

        def block(index, carry):
            at = pl.ds(pl.multiple_of(index * rows, rows), rows)
            normal, _ = norm_parts(tokens[at, :].astype(F32))
            normed[at, :] = (normal * vectors[0:1, :] + vectors[1:2, :]).astype(BF)
            return carry

        lax.fori_loop(0, 13, block, 0)

    zero = jnp.zeros_like(vectors[2:3, :])
    bias = jnp.where(step == 0, vectors[2:3, :], jnp.where(step == 2, vectors[3:4, :], zero))
    qkv[...] = (dot(normed[...], weight[...], 1, 1) + bias).astype(BF)


def qkv_call(tokens, vectors, weight, after=()):
    rows, width = tokens.shape
    return pl.pallas_call(
        waiting(qkv_body, 3, len(after)),
        grid=(3,),
        in_specs=[
            still(rows, width),
            still(16, width),
            pl.BlockSpec((width, width), lambda j: (j, 0)),
        ]
        + [ANYWHERE] * len(after),
        out_specs=[
            pl.BlockSpec((rows, width), lambda j: (0, 0)),
            pl.BlockSpec((rows, width), lambda j: (0, j)),
        ],
        out_shape=[
            jax.ShapeDtypeStruct((rows, width), BF),
            jax.ShapeDtypeStruct((rows, 3 * width), BF),
        ],
        compiler_params=params(),
        cost_estimate=cost(6 * rows * width * width, 2 * (5 * rows * width + 3 * width * width)),
        name="qkv",
    )(tokens, vectors, weight, *after)


def attend_body(first, lengths, qkv, tokens, vectors, weight, _, mixture, middle, normed):
    slots, width = tokens.shape
    live = lax.broadcasted_iota(jnp.int32, (slots, slots), 1) < lengths[pl.program_id(0) + first]
    near = lax.broadcasted_iota(jnp.int32, (slots, 2 * HD), 1) < HD
    for pair in range(H // 2):
        at = 2 * HD * pair
        query = qkv[:, at : at + 2 * HD] * HD**-0.5
        key = qkv[:, width + at : width + at + 2 * HD]
        value = qkv[:, 2 * width + at : 2 * width + at + 2 * HD]
        mixed = []
        for half in (near, ~near):
            scores = dot(jnp.where(half, query, 0), key, 1, 1)
            scores = jnp.where(live, scores, -1e30)
            powers = jnp.exp(scores - jnp.max(scores, axis=1, keepdims=True))
            weights = powers * (1.0 / jnp.sum(powers, axis=1, keepdims=True))
            mixed.append(dot(weights.astype(BF), value, 1, 0))
        mixture[:, at : at + 2 * HD] = jnp.where(near, mixed[0], mixed[1]).astype(BF)
    branch = dot(mixture[...], weight[...], 1, 1)
    middle[...] = branch + (tokens[...].astype(F32) + vectors[4:5, :])
    normal, _ = norm_parts(middle[...])
    normed[...] = (normal * vectors[5:6, :] + vectors[6:7, :]).astype(BF)


def attend_call(lengths, qkv, tokens, vectors, weight, part, parts, earlier=(), after=()):
    rows, width = tokens.shape
    images = lengths.shape[0]
    slots = rows // images
    first = part * images // parts
    spare = list(earlier) + list(after)
    row = pl.BlockSpec((slots, width), lambda i, *_: (i + first, 0))
    return pl.pallas_call(
        waiting(functools.partial(attend_body, first), 6, len(spare)),
        grid_spec=pltpu.PrefetchScalarGridSpec(
            num_scalar_prefetch=1,
            grid=(images // parts,),
            in_specs=[
                pl.BlockSpec((slots, 3 * width), lambda i, *_: (i + first, 0)),
                row,
                still(16, width),
                still(width, width),
            ]
            + [ANYWHERE] * (len(spare) + 1),
            out_specs=[row, row, row],
        ),
        out_shape=[
            jax.ShapeDtypeStruct((rows, width), BF),
            jax.ShapeDtypeStruct((rows, width), F32),
            jax.ShapeDtypeStruct((rows, width), BF),
        ],
        input_output_aliases={6 + place: place for place in range(len(earlier))},
        compiler_params=params(),
        cost_estimate=cost(16 * rows * width * width // parts, 16 * rows * width // parts),
        name="attend",
    )(lengths, qkv, tokens, vectors, weight, lengths, *spare)


def feed_body(hops, begin, chunk, table, normed, cot, up, down, bias, *refs):
    if not begin:
        feed_in, back_in, refs = refs[0], refs[1], refs[2:]
    if hops == 2:
        held_in, refs = refs[0], refs[1:]
    feed, back, bias_grad, refs = refs[0], refs[1], refs[2], refs[3:]
    hidden, slope = refs[-2:]
    slots = normed.shape[0] // 4
    total = jnp.zeros(bias_grad.shape, F32)
    for part in range(4):
        at = slice(slots * part, slots * (part + 1))
        before = dot(normed[at, :], up[...], 1, 1) + bias[8 + chunk : 9 + chunk, :]
        grad = dot(cot[at, :], down[...], 1, 0)
        share, bend = gelu_parts(before)
        hidden[at, :] = (before * share).astype(BF)
        low = (grad * (share + bend)).astype(BF)
        slope[at, :] = low
        total += jnp.sum(low.astype(F32), axis=0, keepdims=True)
        ahead = dot(hidden[at, :], down[...], 1, 1)
        behind = dot(low, up[...], 1, 0)
        feed[at, :] = ahead if begin else feed_in[at, :] + ahead
        back[at, :] = behind if begin else back_in[at, :] + behind
    bias_grad[...] = total
    up_found = dot(slope[...], normed[...], 0, 0)
    down_found = dot(cot[...], hidden[...], 0, 0)
    if not hops:
        refs[0][...] = up_found.astype(BF)
        refs[1][...] = down_found.astype(BF)
        return
    held = refs[0] if hops == 1 else refs[4]
    width = normed.shape[1]
    many = width // 32
    for owner in range(32):
        for place, found in enumerate((up_found, down_found)):
            block = found[many * owner : many * (owner + 1)].reshape(many // 8, 8, width)
            held[owner, many // 8 * place : many // 8 * (place + 1)] = block.astype(BF)
    if hops == 2:
        half = held.shape[1]
        for index in range(32):
            refs[index // 8][index % 8, :half] = held_in[table[index]]
            refs[index // 8][index % 8, half:] = held[table[index]]


def feed_call(chunk, table, normed, cot, up, down, bias, sums=(), held=None, hops=0, after=()):
    rows, width = normed.shape
    spare = list(after)
    begin = not sums
    units = 2 * width // 256
    total = jax.ShapeDtypeStruct((rows, width), F32)
    shapes = [total, total, jax.ShapeDtypeStruct((1, width), F32)]
    scratch = [pltpu.VMEM((rows, width), BF), pltpu.VMEM((rows, width), BF)]
    blocks = (32, units, 8, width)
    if hops == 0:
        shapes += [jax.ShapeDtypeStruct((width, width), BF)] * 2
    elif hops == 1:
        shapes += [jax.ShapeDtypeStruct(blocks, BF)]
    else:
        shapes += group_shapes(2 * units, width)
        scratch = [pltpu.VMEM(blocks, BF)] + scratch
    args = [table, normed, cot, up, down, bias, *sums] + ([held] if hops == 2 else [])
    specs = [pl.BlockSpec(memory_space=pltpu.SMEM)] + [still(*arg.shape) for arg in args[1:]]
    return pl.pallas_call(
        waiting(functools.partial(feed_body, hops, begin, chunk), len(args), len(spare)),
        grid=(1,),
        in_specs=specs + [ANYWHERE] * len(spare),
        out_specs=[still(*shape.shape) for shape in shapes],
        out_shape=shapes,
        scratch_shapes=scratch,
        compiler_params=params(FEED_MIB),
        cost_estimate=cost(12 * rows * width * width, 20 * rows * width + 8 * width * width),
        name="feed",
    )(*args, *spare)


def close_body(middle, cot, vectors, feed, back, output, grad_middle, grad_low, sums):
    slots = output.shape[1]
    behind = back[...]
    values = middle[...]
    given = cot[...].astype(F32)
    output[0] = (values + feed[...] + vectors[7:8, :])[:slots].astype(BF)
    normal, rscale = norm_parts(values)
    grad = given + norm_back(behind * vectors[5:6, :], normal, rscale)
    grad_middle[...] = grad
    low = grad.astype(BF)
    grad_low[...] = low

    @pl.when(pl.program_id(0) == 0)
    def start():
        sums[...] = jnp.zeros_like(sums)

    for place, term in enumerate((behind * normal, behind, given, low.astype(F32))):
        sums[place : place + 1, :] += jnp.sum(term, axis=0, keepdims=True)


def close_call(middle, cot, vectors, feed, back, images, slots, after=()):
    rows, width = middle.shape
    row = pl.BlockSpec((rows // images, width), lambda i: (i, 0))
    fixed = pl.BlockSpec((8, width), lambda i: (0, 0))
    steady = still(16, width)
    return pl.pallas_call(
        waiting(close_body, 5, len(after)),
        grid=(images,),
        in_specs=[row, row, steady, row, row] + [ANYWHERE] * len(after),
        out_specs=[pl.BlockSpec((1, slots, width), lambda i: (i, 0, 0)), row, row, fixed],
        out_shape=[
            jax.ShapeDtypeStruct((images, slots, width), BF),
            jax.ShapeDtypeStruct((rows, width), F32),
            jax.ShapeDtypeStruct((rows, width), BF),
            jax.ShapeDtypeStruct((8, width), F32),
        ],
        compiler_params=params(),
        cost_estimate=cost(5000 * rows * width, 30 * rows * width),
        name="close",
    )(middle, cot, vectors, feed, back, *after)


def attend_back_body(first, lengths, qkv, grad_low, weight, _, grad_qkv, grad_mix):
    slots, width = grad_low.shape
    live = lax.broadcasted_iota(jnp.int32, (slots, slots), 0) < lengths[pl.program_id(0) + first]
    near = lax.broadcasted_iota(jnp.int32, (slots, 2 * HD), 1) < HD
    grad_mix[...] = dot(grad_low[...], weight[...], 1, 0).astype(BF)
    for pair in range(H // 2):
        at = 2 * HD * pair
        query = qkv[:, at : at + 2 * HD] * HD**-0.5
        key = qkv[:, width + at : width + at + 2 * HD]
        value = qkv[:, 2 * width + at : 2 * width + at + 2 * HD]
        mix = grad_mix[:, at : at + 2 * HD]
        found = []
        for half in (near, ~near):
            scores = dot(key, jnp.where(half, query, 0), 1, 1)
            scores = jnp.where(live, scores, -1e30)
            powers = jnp.exp(scores - jnp.max(scores, axis=0, keepdims=True))
            weights = powers * (1.0 / jnp.sum(powers, axis=0, keepdims=True))
            slope = dot(value, jnp.where(half, mix, 0), 1, 1)
            grad_value = dot(weights.astype(BF), mix, 1, 0)
            inner = jnp.sum(slope * weights, axis=0, keepdims=True)
            low = (weights * (slope - inner)).astype(BF)
            grad_key = dot(low, query, 1, 0)
            grad_query = dot(low, key * HD**-0.5, 0, 0)
            found.append((grad_query, grad_key, grad_value))
        for place in range(3):
            grad_qkv[:, place * width + at : place * width + at + 2 * HD] = jnp.where(
                near, found[0][place], found[1][place]
            ).astype(BF)


def attend_back_call(lengths, qkv, grad_low, weight, part, parts, earlier=(), after=()):
    rows, width = grad_low.shape
    images = lengths.shape[0]
    slots = rows // images
    first = part * images // parts
    spare = list(earlier) + list(after)
    wide = pl.BlockSpec((slots, 3 * width), lambda i, *_: (i + first, 0))
    return pl.pallas_call(
        waiting(functools.partial(attend_back_body, first), 5, len(spare)),
        grid_spec=pltpu.PrefetchScalarGridSpec(
            num_scalar_prefetch=1,
            grid=(images // parts,),
            in_specs=[
                wide,
                pl.BlockSpec((slots, width), lambda i, *_: (i + first, 0)),
                still(width, width),
            ]
            + [ANYWHERE] * (1 + len(spare)),
            out_specs=[wide],
            scratch_shapes=[pltpu.VMEM((slots, width), BF)],
        ),
        out_shape=[jax.ShapeDtypeStruct((rows, 3 * width), BF)],
        input_output_aliases={5: 0} if earlier else {},
        compiler_params=params(),
        cost_estimate=cost(30 * rows * width * width // parts, 16 * rows * width // parts),
        name="attend_back",
    )(lengths, qkv, grad_low, weight, lengths, *spare)


def cross_flat_body(left, right, out):
    out[...] = dot(left[...], right[...], 0, 0).astype(BF)


def cross_flat_call(left, right):
    rows, width = right.shape
    wide = left.shape[1]
    return pl.pallas_call(
        cross_flat_body,
        grid=(wide // width,),
        in_specs=[
            pl.BlockSpec((rows, width), lambda j: (0, j)),
            pl.BlockSpec((rows, width), lambda j: (0, 0)),
        ],
        out_specs=pl.BlockSpec((width, width), lambda j: (j, 0)),
        out_shape=jax.ShapeDtypeStruct((wide, width), BF),
        compiler_params=params(),
        cost_estimate=cost(2 * rows * width * wide, 2 * rows * (width + wide) + 2 * wide * width),
        name="cross",
    )(left, right)


def deal(table, held, groups):
    for index in range(32):
        groups[index // 8][index % 8] = held[table[index]]


def group_shapes(units, width):
    return [jax.ShapeDtypeStruct((8, units, 8, width), BF)] * 4


def cross_body(spare, table, left, right, *refs):
    refs = refs[spare:]
    groups, whole, held = refs[:4], refs[4], refs[5]
    step = pl.program_id(0)
    steps = pl.num_programs(0)
    width = right.shape[1]
    for index in range(whole.shape[0] // width):
        @pl.when(step == index)
        def tile():
            whole[width * index : width * (index + 1), :] = dot(left[...], right[...], 0, 0)

    @pl.when(step == steps - 1)
    def last():
        units = held.shape[1]
        for owner in range(32):
            block = whole[8 * units * owner : 8 * units * (owner + 1), :]
            held[owner] = block.reshape(units, 8, width).astype(BF)
        deal(table, held, groups)


def cross_call(table, left, right, after=()):
    rows, width = right.shape
    wide = left.shape[1]
    units = wide // 256
    group = pl.BlockSpec((8, units, 8, width), lambda j, *_: (0, 0, 0, 0))
    return pl.pallas_call(
        functools.partial(cross_body, len(after)),
        grid_spec=pltpu.PrefetchScalarGridSpec(
            num_scalar_prefetch=1,
            grid=(wide // width,),
            in_specs=[
                pl.BlockSpec((rows, width), lambda j, *_: (0, j)),
                pl.BlockSpec((rows, width), lambda j, *_: (0, 0)),
            ]
            + [ANYWHERE] * len(after),
            out_specs=[group] * 4,
            scratch_shapes=[pltpu.VMEM((wide, width), F32), pltpu.VMEM((32, units, 8, width), BF)],
        ),
        out_shape=group_shapes(units, width),
        compiler_params=params(),
        cost_estimate=cost(2 * rows * width * wide, 2 * rows * (width + wide) + 2 * wide * width),
        name="cross",
    )(table, left, right, *after)


def enter_body(
    tokens, grad_qkv, grad_middle, vectors, weight, close_sums, bias0, bias1, bias2, bias3, grad_input, sums
):
    slots, width = grad_input.shape[1:]
    low = grad_qkv[...]
    grad = dot(low, weight[...], 1, 0)
    normal, rscale = norm_parts(tokens[...].astype(F32))
    full = grad_middle[...] + norm_back(grad * vectors[0:1, :], normal, rscale)
    grad_input[0] = full[:slots]

    @pl.when(pl.program_id(0) == 0)
    def start():
        sums[...] = jnp.zeros_like(sums)
        sums[4:8, :] = close_sums[0:4, :]
        for place, bias in enumerate((bias0, bias1, bias2, bias3)):
            sums[8 + place : 9 + place, :] = bias[...]

    query_value = [low[:, :width], low[:, 2 * width :]]
    for place, term in enumerate([grad * normal, grad] + query_value):
        sums[place : place + 1, :] += jnp.sum(term.astype(F32), axis=0, keepdims=True)


def enter_call(tokens, grad_qkv, grad_middle, vectors, weight, close_sums, biases, images, slots, after=()):
    rows, width = tokens.shape
    row = pl.BlockSpec((rows // images, width), lambda i: (i, 0))
    return pl.pallas_call(
        waiting(enter_body, 10, len(after)),
        grid=(images,),
        in_specs=[
            row,
            pl.BlockSpec((rows // images, 3 * width), lambda i: (i, 0)),
            row,
            still(16, width),
            still(3 * width, width),
            still(8, width),
        ]
        + [still(1, width)] * 4
        + [ANYWHERE] * len(after),
        out_specs=[
            pl.BlockSpec((1, slots, width), lambda i: (i, 0, 0)),
            pl.BlockSpec((16, width), lambda i: (0, 0)),
        ],
        out_shape=[
            jax.ShapeDtypeStruct((images, slots, width), F32),
            jax.ShapeDtypeStruct((16, width), F32),
        ],
        compiler_params=params(),
        cost_estimate=cost(6 * rows * width * width, 20 * rows * width),
        name="enter",
    )(tokens, grad_qkv, grad_middle, vectors, weight, close_sums, *biases, *after)


ORDERS = ((8, 16, 2, 4), (16, 8, 4, 2))


def reach(order):
    return [sum(order[bit] for bit in range(4) if index >> bit & 1) for index in range(16)]


def block_table():
    me = lax.axis_index("fsdp")
    near, far = reach(ORDERS[0]), reach(ORDERS[1])
    even = jnp.array(near + [1 ^ place for place in far], jnp.int32)
    odd = jnp.array(far + [1 ^ place for place in near], jnp.int32)
    return jnp.bitwise_xor(jnp.where(me % 2 == 0, even, odd), me.astype(jnp.int32))


def swap(values, step):
    pairs = [(index, index ^ (1 if step < 0 else ORDERS[index % 2][step])) for index in range(32)]
    return lax.ppermute(values, "fsdp", pairs)


def turned(values):
    size = values.shape[1]
    unit = lax.broadcasted_iota(jnp.int32, (size, size), 0) == lax.broadcasted_iota(
        jnp.int32, (size, size), 1
    )
    return dot(unit.astype(BF), values, 1, 1)


def eights(values):
    return values.reshape(values.shape[0] // 8, 8, values.shape[1])


def ready_body(me, rows, lines, out):
    own, width = lines.shape[1], out.shape[3]
    units = rows.shape[0] // 8
    out[0, :units] = eights(rows[...])
    places = lax.broadcasted_iota(jnp.int32, (own, width), 0) + me[0] * own
    spread = (places == lax.broadcasted_iota(jnp.int32, (own, width), 1)).astype(BF)
    out[0, units:] = eights(dot(lines[...], spread, 1, 0)).astype(BF)


def ready_call(me, rows, lines):
    width = rows.shape[1]
    shape = (1, (rows.shape[0] + lines.shape[0]) // 8, 8, width)
    return pl.pallas_call(
        ready_body,
        grid=(1,),
        in_specs=[pl.BlockSpec(memory_space=pltpu.SMEM), still(*rows.shape), still(*lines.shape)],
        out_specs=still(*shape),
        out_shape=jax.ShapeDtypeStruct(shape, BF),
        compiler_params=params(8),
        cost_estimate=cost(0, 1000000),
        name="ready",
    )(me, rows, lines)


def ready_feed_body(up, down, *refs):
    early, late = refs[-2:]
    many = up.shape[0] // CHUNKS
    count = down.shape[0] // (CHUNKS * many)
    own = down.shape[1]
    split = down[...].astype(F32).reshape(count, CHUNKS, many, own)
    for chunk in range(CHUNKS):
        held = turned(split[:, chunk].reshape(count * many, own).astype(BF))
        both = [eights(up[many * chunk : many * (chunk + 1), :].astype(F32)), eights(held)]
        out = early if chunk < CHUNKS // 2 else late
        start = chunk % (CHUNKS // 2) * (many + own) // 8
        out[0, start : start + many // 8] = both[0].astype(BF)
        out[0, start + many // 8 : start + (many + own) // 8] = both[1].astype(BF)


def ready_feed_call(up, down, after):
    width = up.shape[1]
    shape = (1, (up.shape[0] + down.shape[1] * CHUNKS) // 16, 8, width)
    return pl.pallas_call(
        ready_feed_body,
        grid=(1,),
        in_specs=[still(*up.shape), still(*down.shape)] + [ANYWHERE] * len(after),
        out_specs=[still(*shape)] * 2,
        out_shape=[jax.ShapeDtypeStruct(shape, BF)] * 2,
        compiler_params=params(16),
        cost_estimate=cost(0, 1000000),
        name="ready_feed",
    )(up, down, *after)


def pad_body(tokens, cot, *refs):
    for given, out in zip((tokens, cot), refs[-2:]):
        slots = given.shape[1]
        out[...] = jnp.zeros_like(out)
        out[:slots, :] = given[0]


def pad_call(tokens, cot, padded, after=()):
    images, slots, width = tokens.shape
    block = pl.BlockSpec((1, slots, width), lambda i: (i, 0, 0))
    row = pl.BlockSpec((padded, width), lambda i: (i, 0))
    return pl.pallas_call(
        pad_body,
        grid=(images,),
        in_specs=[block, block] + [ANYWHERE] * len(after),
        out_specs=[row, row],
        out_shape=[jax.ShapeDtypeStruct((images * padded, width), BF)] * 2,
        compiler_params=params(16),
        cost_estimate=cost(0, 1000000),
        name="pad",
    )(tokens, cot, *after)


def join_body(left, right, *refs):
    out = refs[-1]
    half = left.shape[0]
    out[:half] = left[...]
    out[half:] = right[...]


def join_call(left, right, after=()):
    shape = (2 * left.shape[0],) + left.shape[1:]
    return pl.pallas_call(
        join_body,
        grid=(1,),
        in_specs=[still(*left.shape), still(*left.shape)] + [ANYWHERE] * len(after),
        out_specs=still(*shape),
        out_shape=jax.ShapeDtypeStruct(shape, BF),
        compiler_params=params(16),
        cost_estimate=cost(0, 100000),
        name="join",
    )(left, right, *after)


def place_body(units, rows, table, *refs):
    groups, parts = refs[:4], refs[-len(units) - (rows > 0) :]
    for index in range(32):
        owner = table[index]
        start = 0
        for part, unit in zip(parts, units):
            part[owner] = groups[index // 8][index % 8, start : start + unit]
            start += unit
    if rows:
        total = jnp.zeros((rows, groups[0].shape[-1]), F32)
        for group in groups:
            for index in range(8):
                total += group[index, start:].astype(F32).reshape(total.shape)
        parts[-1][...] = total


def place_call(table, groups, units, rows=0, after=()):
    width = groups[0].shape[-1]
    shapes = [jax.ShapeDtypeStruct((32, unit, 8, width), BF) for unit in units]
    if rows:
        shapes.append(jax.ShapeDtypeStruct((rows, width), F32))
    return pl.pallas_call(
        functools.partial(place_body, units, rows),
        grid=(1,),
        in_specs=[pl.BlockSpec(memory_space=pltpu.SMEM)]
        + [still(*group.shape) for group in groups]
        + [ANYWHERE] * len(after),
        out_specs=[still(*shape.shape) for shape in shapes],
        out_shape=shapes,
        compiler_params=params(24),
        cost_estimate=cost(0, 4 * 256 * sum(units) * width),
        name="place",
    )(table, *groups, *after)


def sort_body(units, full, *refs):
    parts = refs[-len(units) :]
    start = 0
    for part, unit in zip(parts, units):
        part[...] = full[:, start : start + unit]
        start += unit


def sort_call(full, units, after=()):
    count, unit, _, width = full.shape
    some = 4
    return pl.pallas_call(
        functools.partial(sort_body, units),
        grid=(count // some,),
        in_specs=[pl.BlockSpec((some, unit, 8, width), lambda i: (i, 0, 0, 0))]
        + [ANYWHERE] * len(after),
        out_specs=[pl.BlockSpec((some, part, 8, width), lambda i: (i, 0, 0, 0)) for part in units],
        out_shape=[jax.ShapeDtypeStruct((count, part, 8, width), BF) for part in units],
        compiler_params=params(),
        cost_estimate=cost(0, 4 * 8 * count * unit * width),
        name="sort",
    )(full, *after)


def gather_flat(count, parts):
    width = parts[0].shape[-1]
    full = lax.all_gather(jnp.concatenate(parts, axis=0), "fsdp", axis=0, tiled=True)
    full = full.reshape(count, -1, width)
    found = []
    start = 0
    for part in parts:
        found.append(full[:, start : start + part.shape[0]].reshape(-1, width))
        start += part.shape[0]
    return found


def together(*arrays):
    return lax.optimization_barrier(arrays)


class Scatter:
    def __init__(self, groups):
        self.groups = groups
        self.came = [swap(groups[3], -1), swap(groups[2], -1)]

    def load(self, step):
        if step == 3:
            return (self.groups[1].astype(F32) + self.came[0].astype(F32)).astype(BF)
        return self.total[1 << step :].astype(BF)

    def take(self, step, moved):
        if step == 3:
            self.total = self.groups[0].astype(F32) + self.came[1].astype(F32) + moved.astype(F32)
        else:
            self.total = self.total[: 1 << step] + moved.astype(F32)

    def result(self):
        return self.total.reshape(-1, self.total.shape[-1])


def scatter_flat(parts):
    return [lax.psum_scatter(part.astype(F32), "fsdp", scatter_dimension=0, tiled=True) for part in parts]


def shards(
    count,
    tokens,
    cotangent,
    lengths,
    ln1_gain,
    ln1_bias,
    qkv_weight,
    q_bias,
    v_bias,
    out_weight,
    out_bias,
    ln2_gain,
    ln2_bias,
    up_weight,
    up_bias,
    down_weight,
    down_bias,
):
    images, slots, width = tokens.shape
    hops = count == 32
    padded = -(-slots // 16) * 16
    own = width // count
    units = up_bias.shape[0] // CHUNKS
    table = block_table() if hops else None

    singles = [ln1_gain, ln1_bias, q_bias, v_bias, out_bias, ln2_gain, ln2_bias, down_bias, up_bias]
    if hops:
        me = lax.axis_index("fsdp").astype(jnp.int32)
        qkv_units, out_units, feed_units = width * 3 // 256, width // 256, [width // 256] * 4
        held = qkv_weight.T.reshape(1, qkv_units, 8, width)
        came = swap(held, 0)
        lines = jnp.zeros((16, own), BF).at[:12].set(jnp.concatenate(singles).reshape(12, own))
        out_held = ready_call(me[None], out_weight.T, lines)
        early, late = ready_feed_call(up_weight.T, down_weight, ())
        early_full = lax.all_gather(early.reshape(-1, width), "fsdp", axis=0, tiled=True)
        came, out_held, late = together(came, out_held, late)
        held = join_call(held, came)
        came = swap(held, 1)
        out_came = swap(out_held, 0)
        came, out_came = together(came, out_came)
        held = join_call(held, came)
        came = swap(held, 2)
        out_held = join_call(out_held, out_came)
        out_came = swap(out_held, 1)
        late_came = swap(late, 0)
        came, out_came, late_came = together(came, out_came, late_came)
        held = join_call(held, came)
        across = swap(held, -1)
        came = swap(held, 3)
        out_held = join_call(out_held, out_came)
        out_came = swap(out_held, 2)
        late = join_call(late, late_came)
        late_came = swap(late, 1)
        token_rows, cot_rows = pad_call(tokens, cotangent, padded)
        out_came, token_rows, cot_rows = together(out_came, token_rows, cot_rows)
        out_held = join_call(out_held, out_came)
        out_across = swap(out_held, -1)
        out_came = swap(out_held, 3)
        came, out_came, late_came = together(came, out_came, late_came)
        came_across = swap(came, -1)
        out_came_across = swap(out_came, -1)
        late = join_call(late, late_came)
        late_came = swap(late, 2)
        out_full, vectors = place_call(
            table, (out_held, out_came, out_across, out_came_across), [out_units], 16
        )
        (qkv_full,) = place_call(table, (held, came, across, came_across), [qkv_units])
        qkv_full, out_full = qkv_full.reshape(-1, width), out_full.reshape(-1, width)
    else:
        down_rows = down_weight.reshape(count, CHUNKS, units, own).transpose(1, 3, 0, 2)
        down_rows = down_rows.reshape(CHUNKS, own, width)
        up_rows = up_weight.T.reshape(CHUNKS, units, width)
        vector = jnp.concatenate(singles)
        extra = jnp.zeros((8, width), BF).at[0, : vector.shape[0]].set(vector)
        qkv_full, extra, out_full = gather_flat(count, [qkv_weight.T, extra, out_weight.T])
        up_full = gather_flat(count, [up_rows[chunk] for chunk in range(CHUNKS)])
        down_full = gather_flat(count, [down_rows[chunk] for chunk in range(CHUNKS)])
        extra = extra.reshape(count, 8, width)[:, 0, : vector.shape[0]].astype(F32)
        vectors = extra.reshape(count, 12, own).transpose(1, 0, 2).reshape(12, width)
        vectors = jnp.pad(vectors, ((0, 4), (0, 0)))
        token_rows, cot_rows = pad_call(tokens, cotangent, padded)

    normed_one, qkv = qkv_call(token_rows, vectors, qkv_full)
    if hops:
        qkv, late_came = together(qkv, late_came)
        late = join_call(late, late_came)
        late_across = swap(late, -1)
        late_came = swap(late, 3)
    found = attend_call(lengths, qkv, token_rows, vectors, out_full, 0, 2)
    found = attend_call(lengths, qkv, token_rows, vectors, out_full, 1, 2, found)
    mixture, middle, normed_two = found
    if hops:
        (early_full, normed_two) = together(early_full, normed_two)
        full = early_full.reshape(32, sum(feed_units), 8, width)
        rest = [part.reshape(width, width) for part in sort_call(full, feed_units)]
        up_full, down_full = rest[0::2], rest[1::2]

    bias_grads, sums, totals, held = [], [], (), None
    chains = []
    for chunk in range(CHUNKS):
        kind = (1 + chunk % 2) if hops else 0
        feed, back, bias_grad, *found = feed_call(
            chunk,
            table if hops else lengths,
            normed_two,
            cot_rows,
            up_full[chunk],
            down_full[chunk],
            vectors,
            totals,
            held,
            kind,
        )
        if not hops:
            sums.append(jnp.concatenate(scatter_flat(found)))
        elif chunk == 0:
            held = found[0]
            feed, late_came, late_across = together(feed, late_came, late_across)
            late_came_across = swap(late_came, -1)
        elif chunk == 1:
            held = None
            feed, late_came_across = together(feed, late_came_across)
            first = Scatter(found)
            groups = (late, late_came, late_across, late_came_across)
            rest = [part.reshape(width, width) for part in place_call(table, groups, feed_units)]
            up_full, down_full = up_full + rest[0::2], down_full + rest[1::2]
            *first.came, feed = together(*first.came, feed)
        elif chunk == 2:
            held = found[0]
            load, feed = together(first.load(3), feed)
            moved = swap(load, 3)
        else:
            second = Scatter(found)
            feed, moved = together(feed, moved)
        totals = (feed, back)
        bias_grads.append(bias_grad)
    output, grad_middle, grad_low, close_sums = close_call(
        middle, cot_rows, vectors, feed, back, images, slots
    )
    if hops:
        moved, grad_low, *second.came = together(moved, grad_low, *second.came)
        first.take(3, moved)
        load, load_two, grad_low = together(first.load(2), second.load(3), grad_low)
        moved = swap(load, 2)
        moved_two = swap(load_two, 3)
        outs = Scatter(cross_call(table, grad_low, mixture))
        found = attend_back_call(lengths, qkv, grad_low, out_full, 0, 2)
        grad_qkv, moved, *outs.came = together(found[0], moved, *outs.came)
        first.take(2, moved)
        load, load_out, grad_qkv = together(first.load(1), outs.load(3), grad_qkv)
        moved = swap(load, 1)
        moved_out = swap(load_out, 3)
        found = attend_back_call(lengths, qkv, grad_low, out_full, 1, 2, [grad_qkv])
        grad_qkv, moved, moved_out, moved_two = together(found[0], moved, moved_out, moved_two)
        first.take(1, moved)
        second.take(3, moved_two)
        outs.take(3, moved_out)
        load, load_two, load_out, grad_qkv = together(
            first.load(0), second.load(2), outs.load(2), grad_qkv
        )
        moved_two = swap(load_two, 2)
        moved_out = swap(load_out, 2)
        moved = swap(load, 0)
        last = Scatter(cross_call(table, grad_qkv, normed_one))
        load, grad_qkv = together(last.load(3), grad_qkv)
        moved_last = swap(load, 3)
    else:
        (out_sum,) = scatter_flat([cross_flat_call(grad_low, mixture)])
        (grad_qkv,) = attend_back_call(lengths, qkv, grad_low, out_full, 0, 1)
        (qkv_sum,) = scatter_flat([cross_flat_call(grad_qkv, normed_one)])
    grad_input, vector_sums = enter_call(
        token_rows, grad_qkv, grad_middle, vectors, qkv_full, close_sums, bias_grads, images, slots
    )
    if hops:
        vector_sums, moved, moved_out, moved_two = together(vector_sums, moved, moved_out, moved_two)
        first.take(0, moved)
        second.take(2, moved_two)
        outs.take(2, moved_out)
        vector_sums += swap(vector_sums, -1)
        moved_two = swap(second.load(1), 1)
        moved_out = swap(outs.load(1), 1)
        moved_vec = swap(vector_sums, 3)
        moved_last, moved_vec, moved_two, moved_out = together(
            moved_last, moved_vec, moved_two, moved_out
        )
        last.take(3, moved_last)
        vector_sums += moved_vec
        second.take(1, moved_two)
        outs.take(1, moved_out)
        load, load_vec = together(last.load(2), vector_sums)
        moved_vec = swap(load_vec, 2)
        moved_last = swap(load, 2)
        moved_two = swap(second.load(0), 0)
        moved_out = swap(outs.load(0), 0)
        moved_last, moved_vec = together(moved_last, moved_vec)
        for step in (1, 0):
            last.take(step + 1, moved_last)
            vector_sums += moved_vec
            moved_vec = swap(vector_sums, step)
            moved_last = swap(last.load(step), step)
            if step:
                moved_last, moved_vec, moved_two, moved_out = together(
                    moved_last, moved_vec, moved_two, moved_out
                )
                second.take(0, moved_two)
                outs.take(0, moved_out)
        last.take(0, moved_last)
        vector_sums += moved_vec
        for chain in (first, second):
            found = chain.result()
            sums += [found[: 2 * own], found[2 * own :]]
        qkv_sum, out_sum = last.result(), outs.result()
    else:
        vector_sums = lax.psum(vector_sums, "fsdp")
    place = lax.axis_index("fsdp") * own
    vector_sums = lax.dynamic_slice(vector_sums, (0, place), (16, own))
    vec = [vector_sums[row] for row in (0, 1, 2, 3, 7, 4, 5, 6)]

    up_sum = jnp.concatenate([found[:units] for found in sums]).T
    down_sum = jnp.stack([found[units:] for found in sums]).reshape(CHUNKS, own, count, units)
    down_sum = down_sum.transpose(2, 0, 3, 1).reshape(count * CHUNKS * units, own)
    return (
        output,
        grad_input,
        vec[0],
        vec[1],
        qkv_sum.T,
        vec[2],
        vec[3],
        out_sum.T,
        vec[4],
        vec[5],
        vec[6],
        up_sum,
        vector_sums[8:12].reshape(-1),
        down_sum,
        vec[7],
    )


def solution(mesh):
    row, column, vector = P("fsdp", None, None), P(None, "fsdp"), P("fsdp")
    return jax.shard_map(
        functools.partial(shards, mesh.shape["fsdp"]),
        mesh=mesh,
        in_specs=(row, row, vector, vector, vector, column, vector, vector, column, vector)
        + (vector, vector, column, vector, column, vector),
        out_specs=(row, row, vector, vector, column, vector, vector, column, vector)
        + (vector, vector, column, vector, column, vector),
        check_vma=False,
    )
```

```python
import functools

import jax
import jax.numpy as jnp
from jax import lax
from jax.experimental import pallas as pl
from jax.experimental.pallas import tpu as pltpu
from jax.sharding import PartitionSpec as P

H = 12
HD = 64
EPS = 1e-06
BF = jnp.bfloat16
F32 = jnp.float32
MIB = 1024 * 1024
CHUNKS = 4
COST = 8
FEED_MIB = 54


def dot(left, right, left_dim, right_dim):
    return lax.dot_general(
        left, right, (((left_dim,), (right_dim,)), ((), ())), preferred_element_type=F32
    )


def norm_parts(values):
    center = values - jnp.mean(values, axis=-1, keepdims=True)
    rscale = lax.rsqrt(jnp.mean(center * center, axis=-1, keepdims=True) + EPS)
    return center * rscale, rscale


def norm_back(grad_normal, normal, rscale):
    grad_mean = jnp.mean(grad_normal, axis=-1, keepdims=True)
    grad_cross = jnp.mean(grad_normal * normal, axis=-1, keepdims=True)
    return rscale * (grad_normal - grad_mean - normal * grad_cross)


def gelu_parts(values):
    size = jnp.abs(values)
    step = 1.0 / (1.0 + (0.3275911 * 0.7071067811865476) * size)
    bell = jnp.exp(-0.5 * values * values)
    poly = 1.061405429 * 0.5
    for factor in (-1.453152027, 1.421413741, -0.284496736, 0.254829592):
        poly = poly * step + 0.5 * factor
    tail = poly * step * bell
    return jnp.where(values >= 0, 1.0 - tail, tail), values * bell * 0.3989422804014327


def params(mib=24):
    return pltpu.CompilerParams(vmem_limit_bytes=mib * MIB)


def waiting(body, inputs, spare):
    return lambda *refs: body(*refs[:inputs], *refs[inputs + spare :])


ANYWHERE = pl.BlockSpec(memory_space=pl.ANY)


def cost(flops, moved):
    return pl.CostEstimate(flops=flops // COST, bytes_accessed=moved // COST, transcendentals=0)


def still(*shape):
    return pl.BlockSpec(shape, lambda *_: (0,) * len(shape), pipeline_mode=pl.Buffered(1))


def qkv_body(kinds, table, tokens, vectors, *refs):
    weights, refs = refs[:kinds], refs[kinds:]
    normed, qkv = refs[:2]
    step = pl.program_id(0)
    width = tokens.shape[1]

    @pl.when(step == 0)
    def first():
        if kinds > 1:
            full, held = refs[2:]
            for index in range(32):
                held[table[index]] = weights[index // 8][index % 8]
            full[...] = held[...].reshape(full.shape)
        rows = normed.shape[0] // 13

        def block(index, carry):
            at = pl.ds(pl.multiple_of(index * rows, rows), rows)
            normal, _ = norm_parts(tokens[at, :].astype(F32))
            normed[at, :] = (normal * vectors[0:1, :] + vectors[1:2, :]).astype(BF)
            return carry

        lax.fori_loop(0, 13, block, 0)

    full = refs[2] if kinds > 1 else weights[0]
    weight = full[pl.ds(pl.multiple_of(step * width, width), width), :]
    zero = jnp.zeros_like(vectors[2:3, :])
    bias = jnp.where(step == 0, vectors[2:3, :], jnp.where(step == 2, vectors[3:4, :], zero))
    qkv[...] = (dot(normed[...], weight, 1, 1) + bias).astype(BF)


def qkv_call(table, tokens, vectors, weights):
    rows, width = tokens.shape
    grouped = len(weights) > 1
    specs = [pl.BlockSpec((rows, width), lambda j: (0, 0)), pl.BlockSpec((rows, width), lambda j: (0, j))]
    shapes = [jax.ShapeDtypeStruct((rows, width), BF), jax.ShapeDtypeStruct((rows, 3 * width), BF)]
    if grouped:
        specs.append(still(3 * width, width))
        shapes.append(jax.ShapeDtypeStruct((3 * width, width), BF))
    return pl.pallas_call(
        functools.partial(qkv_body, len(weights)),
        grid=(3,),
        in_specs=[pl.BlockSpec(memory_space=pltpu.SMEM), still(rows, width), still(16, width)]
        + [still(*array.shape) for array in weights],
        out_specs=specs,
        out_shape=shapes,
        scratch_shapes=[pltpu.VMEM((32, 3 * width // 256, 8, width), BF)] if grouped else [],
        compiler_params=params(),
        cost_estimate=cost(6 * rows * width * width, 2 * (5 * rows * width + 3 * width * width)),
        name="qkv",
    )(table, tokens, vectors, *weights)


def attend_body(first, lengths, qkv, tokens, vectors, weight, _, mixture, middle, normed):
    slots, width = tokens.shape
    live = lax.broadcasted_iota(jnp.int32, (slots, slots), 1) < lengths[pl.program_id(0) + first]
    near = lax.broadcasted_iota(jnp.int32, (slots, 2 * HD), 1) < HD
    for pair in range(H // 2):
        at = 2 * HD * pair
        query = qkv[:, at : at + 2 * HD] * HD**-0.5
        key = qkv[:, width + at : width + at + 2 * HD]
        value = qkv[:, 2 * width + at : 2 * width + at + 2 * HD]
        mixed = []
        for half in (near, ~near):
            scores = dot(jnp.where(half, query, 0), key, 1, 1)
            scores = jnp.where(live, scores, -1e30)
            powers = jnp.exp(scores - jnp.max(scores, axis=1, keepdims=True))
            weights = powers * (1.0 / jnp.sum(powers, axis=1, keepdims=True))
            mixed.append(dot(weights.astype(BF), value, 1, 0))
        mixture[:, at : at + 2 * HD] = jnp.where(near, mixed[0], mixed[1]).astype(BF)
    branch = dot(mixture[...], weight[...], 1, 1)
    middle[...] = branch + (tokens[...].astype(F32) + vectors[4:5, :])
    normal, _ = norm_parts(middle[...])
    normed[...] = (normal * vectors[5:6, :] + vectors[6:7, :]).astype(BF)


def attend_call(lengths, qkv, tokens, vectors, weight, part, parts, earlier=(), after=()):
    rows, width = tokens.shape
    images = lengths.shape[0]
    slots = rows // images
    first = part * images // parts
    spare = list(earlier) + list(after)
    row = pl.BlockSpec((slots, width), lambda i, *_: (i + first, 0))
    return pl.pallas_call(
        waiting(functools.partial(attend_body, first), 6, len(spare)),
        grid_spec=pltpu.PrefetchScalarGridSpec(
            num_scalar_prefetch=1,
            grid=(images // parts,),
            in_specs=[
                pl.BlockSpec((slots, 3 * width), lambda i, *_: (i + first, 0)),
                row,
                still(16, width),
                still(width, width),
            ]
            + [ANYWHERE] * (len(spare) + 1),
            out_specs=[row, row, row],
        ),
        out_shape=[
            jax.ShapeDtypeStruct((rows, width), BF),
            jax.ShapeDtypeStruct((rows, width), F32),
            jax.ShapeDtypeStruct((rows, width), BF),
        ],
        input_output_aliases={6 + place: place for place in range(len(earlier))},
        compiler_params=params(),
        cost_estimate=cost(16 * rows * width * width // parts, 16 * rows * width // parts),
        name="attend",
    )(lengths, qkv, tokens, vectors, weight, lengths, *spare)


def close_rows(values, total, behind, given, vectors):
    normal, rscale = norm_parts(values)
    grad = given + norm_back(behind * vectors[5:6, :], normal, rscale)
    low = grad.astype(BF)
    return values + total + vectors[7:8, :], grad, low, (behind * normal, behind, given, low.astype(F32))


def feed_body(hops, begin, chunk, table, normed, cot, bias, *refs):
    tiles = 2 if hops else 1
    close = hops and not begin
    weights, refs = refs[: 2 * tiles], refs[2 * tiles :]
    if not begin:
        feed_in, back_in, refs = refs[0], refs[1], refs[2:]
    if close:
        middle, mixture, output, grad_middle, grad_low, sums, *refs = refs
        sums[...] = jnp.zeros_like(sums)
    else:
        feed, back, *refs = refs
    bias_grad, *refs = refs
    hidden, slope = refs[-2:]
    slots = normed.shape[0] // 4
    width = normed.shape[1]
    if hops:
        groups, held, flat = refs[:4], refs[4], refs[5]
        units = weights[0].shape[1] // 4
        for index in range(32):
            held[table[index], : 4 * units] = weights[index // 8][index % 8]
        for place in range(4):
            flat[place] = held[:, units * place : units * (place + 1)].reshape(width, width)
    for part in range(4):
        at = slice(slots * part, slots * (part + 1))
        ahead = 0.0 if begin else feed_in[at, :]
        behind = 0.0 if begin else back_in[at, :]
        for tile in range(tiles):
            up = flat[2 * tile] if hops else weights[0][...]
            down = flat[2 * tile + 1] if hops else weights[1][...]
            row = 8 + chunk + tile
            before = dot(normed[at, :], up, 1, 1) + bias[row : row + 1, :]
            grad = dot(cot[at, :], down, 1, 0)
            share, bend = gelu_parts(before)
            hidden[tile, at, :] = (before * share).astype(BF)
            low = (grad * (share + bend)).astype(BF)
            slope[tile, at, :] = low
            total = jnp.sum(low.astype(F32), axis=0, keepdims=True)
            if part == 0:
                bias_grad[tile : tile + 1, :] = total
            else:
                bias_grad[tile : tile + 1, :] += total
            ahead += dot(hidden[tile, at, :], down, 1, 1)
            behind += dot(low, up, 1, 0)
        if not close:
            feed[at, :] = ahead
            back[at, :] = behind
            continue
        result, grad, low, terms = close_rows(
            middle[at, :], ahead, behind, cot[at, :].astype(F32), bias
        )
        output[part] = result[: output.shape[1]].astype(BF)
        grad_middle[at, :] = grad
        grad_low[at, :] = low
        for place, term in enumerate(terms):
            sums[place : place + 1, :] += jnp.sum(term, axis=0, keepdims=True)
    if close:
        found = dot(grad_low[...], mixture[...], 0, 0)
        for owner in range(32):
            block = found[8 * units * owner : 8 * units * (owner + 1)]
            held[owner, 4 * units :] = eights(block).astype(BF)
    for tile in range(tiles):
        found = [dot(slope[tile], normed[...], 0, 0), dot(cot[...], hidden[tile], 0, 0)]
        if not hops:
            refs[0][...] = found[0].astype(BF)
            refs[1][...] = found[1].astype(BF)
            return
        for owner in range(32):
            for place in range(2):
                block = found[place][8 * units * owner : 8 * units * (owner + 1)]
                spot = units * (2 * tile + place)
                held[owner, spot : spot + units] = eights(block).astype(BF)
    deal(table, held, groups)


def feed_call(chunk, table, normed, cot, weights, vectors, sums=(), hops=False, ends=(), slots=0):
    rows, width = normed.shape
    tiles = 2 if hops else 1
    total = jax.ShapeDtypeStruct((rows, width), F32)
    if ends:
        shapes = [
            jax.ShapeDtypeStruct((4, slots, width), BF),
            total,
            jax.ShapeDtypeStruct((rows, width), BF),
            jax.ShapeDtypeStruct((8, width), F32),
        ]
    else:
        shapes = [total, total]
    shapes.append(jax.ShapeDtypeStruct((tiles, width), F32))
    scratch = [pltpu.VMEM((tiles, rows, width), BF)] * 2
    if hops:
        units = (5 if ends else 4) * width // 256
        shapes += group_shapes(units, width)
        held = [pltpu.VMEM((32, units, 8, width), BF), pltpu.VMEM((4, width, width), BF)]
        scratch = held + scratch
    else:
        shapes += [jax.ShapeDtypeStruct((width, width), BF)] * 2
    arrays = [normed, cot, vectors, *weights, *sums, *ends]
    return pl.pallas_call(
        functools.partial(feed_body, hops, not sums, chunk),
        grid=(1,),
        in_specs=[pl.BlockSpec(memory_space=pltpu.SMEM)] + [still(*array.shape) for array in arrays],
        out_specs=[still(*shape.shape) for shape in shapes],
        out_shape=shapes,
        scratch_shapes=scratch,
        compiler_params=params(FEED_MIB),
        cost_estimate=cost(12 * tiles * rows * width * width, 20 * rows * width),
        name="feed",
    )(table, *arrays)


def close_body(middle, cot, vectors, feed, back, output, grad_middle, grad_low, sums):
    result, grad, low, terms = close_rows(
        middle[...], feed[...], back[...], cot[...].astype(F32), vectors
    )
    output[0] = result[: output.shape[1]].astype(BF)
    grad_middle[...] = grad
    grad_low[...] = low

    @pl.when(pl.program_id(0) == 0)
    def start():
        sums[...] = jnp.zeros_like(sums)

    for place, term in enumerate(terms):
        sums[place : place + 1, :] += jnp.sum(term, axis=0, keepdims=True)


def close_call(middle, cot, vectors, feed, back, images, slots, after=()):
    rows, width = middle.shape
    row = pl.BlockSpec((rows // images, width), lambda i: (i, 0))
    fixed = pl.BlockSpec((8, width), lambda i: (0, 0))
    steady = still(16, width)
    return pl.pallas_call(
        waiting(close_body, 5, len(after)),
        grid=(images,),
        in_specs=[row, row, steady, row, row] + [ANYWHERE] * len(after),
        out_specs=[pl.BlockSpec((1, slots, width), lambda i: (i, 0, 0)), row, row, fixed],
        out_shape=[
            jax.ShapeDtypeStruct((images, slots, width), BF),
            jax.ShapeDtypeStruct((rows, width), F32),
            jax.ShapeDtypeStruct((rows, width), BF),
            jax.ShapeDtypeStruct((8, width), F32),
        ],
        compiler_params=params(),
        cost_estimate=cost(5000 * rows * width, 30 * rows * width),
        name="close",
    )(middle, cot, vectors, feed, back, *after)


def attend_back_body(first, lengths, qkv, grad_low, weight, _, grad_qkv, grad_mix):
    slots, width = grad_low.shape
    live = lax.broadcasted_iota(jnp.int32, (slots, slots), 0) < lengths[pl.program_id(0) + first]
    near = lax.broadcasted_iota(jnp.int32, (slots, 2 * HD), 1) < HD
    grad_mix[...] = dot(grad_low[...], weight[...], 1, 0).astype(BF)
    for pair in range(H // 2):
        at = 2 * HD * pair
        query = qkv[:, at : at + 2 * HD] * HD**-0.5
        key = qkv[:, width + at : width + at + 2 * HD]
        value = qkv[:, 2 * width + at : 2 * width + at + 2 * HD]
        mix = grad_mix[:, at : at + 2 * HD]
        found = []
        for half in (near, ~near):
            scores = dot(key, jnp.where(half, query, 0), 1, 1)
            scores = jnp.where(live, scores, -1e30)
            powers = jnp.exp(scores - jnp.max(scores, axis=0, keepdims=True))
            weights = powers * (1.0 / jnp.sum(powers, axis=0, keepdims=True))
            slope = dot(value, jnp.where(half, mix, 0), 1, 1)
            grad_value = dot(weights.astype(BF), mix, 1, 0)
            inner = jnp.sum(slope * weights, axis=0, keepdims=True)
            low = (weights * (slope - inner)).astype(BF)
            grad_key = dot(low, query, 1, 0)
            grad_query = dot(low, key * HD**-0.5, 0, 0)
            found.append((grad_query, grad_key, grad_value))
        for place in range(3):
            grad_qkv[:, place * width + at : place * width + at + 2 * HD] = jnp.where(
                near, found[0][place], found[1][place]
            ).astype(BF)


def attend_back_call(lengths, qkv, grad_low, weight, part, parts, earlier=(), after=()):
    rows, width = grad_low.shape
    images = lengths.shape[0]
    slots = rows // images
    first = part * images // parts
    spare = list(earlier) + list(after)
    wide = pl.BlockSpec((slots, 3 * width), lambda i, *_: (i + first, 0))
    return pl.pallas_call(
        waiting(functools.partial(attend_back_body, first), 5, len(spare)),
        grid_spec=pltpu.PrefetchScalarGridSpec(
            num_scalar_prefetch=1,
            grid=(images // parts,),
            in_specs=[
                wide,
                pl.BlockSpec((slots, width), lambda i, *_: (i + first, 0)),
                still(width, width),
            ]
            + [ANYWHERE] * (1 + len(spare)),
            out_specs=[wide],
            scratch_shapes=[pltpu.VMEM((slots, width), BF)],
        ),
        out_shape=[jax.ShapeDtypeStruct((rows, 3 * width), BF)],
        input_output_aliases={5: 0} if earlier else {},
        compiler_params=params(),
        cost_estimate=cost(30 * rows * width * width // parts, 16 * rows * width // parts),
        name="attend_back",
    )(lengths, qkv, grad_low, weight, lengths, *spare)


def cross_flat_body(left, right, out):
    out[...] = dot(left[...], right[...], 0, 0).astype(BF)


def cross_flat_call(left, right):
    rows, width = right.shape
    wide = left.shape[1]
    return pl.pallas_call(
        cross_flat_body,
        grid=(wide // width,),
        in_specs=[
            pl.BlockSpec((rows, width), lambda j: (0, j)),
            pl.BlockSpec((rows, width), lambda j: (0, 0)),
        ],
        out_specs=pl.BlockSpec((width, width), lambda j: (j, 0)),
        out_shape=jax.ShapeDtypeStruct((wide, width), BF),
        compiler_params=params(),
        cost_estimate=cost(2 * rows * width * wide, 2 * rows * (width + wide) + 2 * wide * width),
        name="cross",
    )(left, right)


def deal(table, held, groups):
    for index in range(32):
        groups[index // 8][index % 8] = held[table[index]]


def group_shapes(units, width):
    return [jax.ShapeDtypeStruct((8, units, 8, width), BF)] * 4


def cross_body(spare, table, left, right, *refs):
    refs = refs[spare:]
    groups, whole, held = refs[:4], refs[4], refs[5]
    step = pl.program_id(0)
    steps = pl.num_programs(0)
    width = right.shape[1]
    for index in range(whole.shape[0] // width):
        @pl.when(step == index)
        def tile():
            whole[width * index : width * (index + 1), :] = dot(left[...], right[...], 0, 0)

    @pl.when(step == steps - 1)
    def last():
        units = held.shape[1]
        for owner in range(32):
            block = whole[8 * units * owner : 8 * units * (owner + 1), :]
            held[owner] = block.reshape(units, 8, width).astype(BF)
        deal(table, held, groups)


def cross_call(table, left, right, after=()):
    rows, width = right.shape
    wide = left.shape[1]
    units = wide // 256
    group = pl.BlockSpec((8, units, 8, width), lambda j, *_: (0, 0, 0, 0))
    return pl.pallas_call(
        functools.partial(cross_body, len(after)),
        grid_spec=pltpu.PrefetchScalarGridSpec(
            num_scalar_prefetch=1,
            grid=(wide // width,),
            in_specs=[
                pl.BlockSpec((rows, width), lambda j, *_: (0, j)),
                pl.BlockSpec((rows, width), lambda j, *_: (0, 0)),
            ]
            + [ANYWHERE] * len(after),
            out_specs=[group] * 4,
            scratch_shapes=[pltpu.VMEM((wide, width), F32), pltpu.VMEM((32, units, 8, width), BF)],
        ),
        out_shape=group_shapes(units, width),
        compiler_params=params(),
        cost_estimate=cost(2 * rows * width * wide, 2 * rows * (width + wide) + 2 * wide * width),
        name="cross",
    )(table, left, right, *after)


def enter_body(tokens, grad_qkv, grad_middle, vectors, weight, close_sums, *refs):
    biases, (grad_input, sums) = refs[:-2], refs[-2:]
    slots, width = grad_input.shape[1:]
    low = grad_qkv[...]
    grad = dot(low, weight[...], 1, 0)
    normal, rscale = norm_parts(tokens[...].astype(F32))
    full = grad_middle[...] + norm_back(grad * vectors[0:1, :], normal, rscale)
    grad_input[0] = full[:slots]

    @pl.when(pl.program_id(0) == 0)
    def start():
        sums[...] = jnp.zeros_like(sums)
        sums[4:8, :] = close_sums[0:4, :]
        each = biases[0].shape[0]
        for place, bias in enumerate(biases):
            sums[8 + each * place : 8 + each * (place + 1), :] = bias[...]

    query_value = [low[:, :width], low[:, 2 * width :]]
    for place, term in enumerate([grad * normal, grad] + query_value):
        sums[place : place + 1, :] += jnp.sum(term.astype(F32), axis=0, keepdims=True)


def enter_call(tokens, grad_qkv, grad_middle, vectors, weight, close_sums, biases, images, slots):
    rows, width = tokens.shape
    row = pl.BlockSpec((rows // images, width), lambda i: (i, 0))
    return pl.pallas_call(
        enter_body,
        grid=(images,),
        in_specs=[
            row,
            pl.BlockSpec((rows // images, 3 * width), lambda i: (i, 0)),
            row,
            still(16, width),
            still(3 * width, width),
            still(8, width),
        ]
        + [still(*bias.shape) for bias in biases],
        out_specs=[
            pl.BlockSpec((1, slots, width), lambda i: (i, 0, 0)),
            pl.BlockSpec((16, width), lambda i: (0, 0)),
        ],
        out_shape=[
            jax.ShapeDtypeStruct((images, slots, width), F32),
            jax.ShapeDtypeStruct((16, width), F32),
        ],
        compiler_params=params(),
        cost_estimate=cost(6 * rows * width * width, 20 * rows * width),
        name="enter",
    )(tokens, grad_qkv, grad_middle, vectors, weight, close_sums, *biases)


ORDERS = ((8, 16, 2, 4), (16, 8, 4, 2))


def reach(order):
    return [sum(order[bit] for bit in range(4) if index >> bit & 1) for index in range(16)]


def block_table():
    me = lax.axis_index("fsdp")
    near, far = reach(ORDERS[0]), reach(ORDERS[1])
    even = jnp.array(near + [1 ^ place for place in far], jnp.int32)
    odd = jnp.array(far + [1 ^ place for place in near], jnp.int32)
    return jnp.bitwise_xor(jnp.where(me % 2 == 0, even, odd), me.astype(jnp.int32))


def swap(values, step):
    pairs = []
    for index in range(32):
        order = ORDERS[index % 2]
        flip = 1 if step == -1 else order[0] ^ order[1] if step == -2 else order[step]
        pairs.append((index, index ^ flip))
    return lax.ppermute(values, "fsdp", pairs)


def turned(values):
    size = values.shape[1]
    unit = lax.broadcasted_iota(jnp.int32, (size, size), 0) == lax.broadcasted_iota(
        jnp.int32, (size, size), 1
    )
    return dot(unit.astype(BF), values, 1, 1)


def eights(values):
    return values.reshape(values.shape[0] // 8, 8, values.shape[1])


def ready_body(me, rows, lines, out):
    own, width = lines.shape[1], out.shape[3]
    units = rows.shape[0] // 8
    out[0, :units] = eights(rows[...])
    places = lax.broadcasted_iota(jnp.int32, (own, width), 0) + me[0] * own
    spread = (places == lax.broadcasted_iota(jnp.int32, (own, width), 1)).astype(BF)
    out[0, units:] = eights(dot(lines[...], spread, 1, 0)).astype(BF)


def ready_call(me, rows, lines):
    width = rows.shape[1]
    shape = (1, (rows.shape[0] + lines.shape[0]) // 8, 8, width)
    return pl.pallas_call(
        ready_body,
        grid=(1,),
        in_specs=[pl.BlockSpec(memory_space=pltpu.SMEM), still(*rows.shape), still(*lines.shape)],
        out_specs=still(*shape),
        out_shape=jax.ShapeDtypeStruct(shape, BF),
        compiler_params=params(8),
        cost_estimate=cost(0, 1000000),
        name="ready",
    )(me, rows, lines)


def ready_feed_body(up, down, *refs):
    early, late = refs[-2:]
    many = up.shape[0] // CHUNKS
    count = down.shape[0] // (CHUNKS * many)
    own = down.shape[1]
    split = down[...].astype(F32).reshape(count, CHUNKS, many, own)
    for chunk in range(CHUNKS):
        held = turned(split[:, chunk].reshape(count * many, own).astype(BF))
        both = [eights(up[many * chunk : many * (chunk + 1), :].astype(F32)), eights(held)]
        out = early if chunk < CHUNKS // 2 else late
        start = chunk % (CHUNKS // 2) * (many + own) // 8
        out[0, start : start + many // 8] = both[0].astype(BF)
        out[0, start + many // 8 : start + (many + own) // 8] = both[1].astype(BF)


def ready_feed_call(up, down, after):
    width = up.shape[1]
    shape = (1, (up.shape[0] + down.shape[1] * CHUNKS) // 16, 8, width)
    return pl.pallas_call(
        ready_feed_body,
        grid=(1,),
        in_specs=[still(*up.shape), still(*down.shape)] + [ANYWHERE] * len(after),
        out_specs=[still(*shape)] * 2,
        out_shape=[jax.ShapeDtypeStruct(shape, BF)] * 2,
        compiler_params=params(16),
        cost_estimate=cost(0, 1000000),
        name="ready_feed",
    )(up, down, *after)


def pad_body(tokens, cot, *refs):
    for given, out in zip((tokens, cot), refs[-2:]):
        slots = given.shape[1]
        out[...] = jnp.zeros_like(out)
        out[:slots, :] = given[0]


def pad_call(tokens, cot, padded, after=()):
    images, slots, width = tokens.shape
    block = pl.BlockSpec((1, slots, width), lambda i: (i, 0, 0))
    row = pl.BlockSpec((padded, width), lambda i: (i, 0))
    return pl.pallas_call(
        pad_body,
        grid=(images,),
        in_specs=[block, block] + [ANYWHERE] * len(after),
        out_specs=[row, row],
        out_shape=[jax.ShapeDtypeStruct((images * padded, width), BF)] * 2,
        compiler_params=params(16),
        cost_estimate=cost(0, 1000000),
        name="pad",
    )(tokens, cot, *after)


def join_body(*refs):
    out = refs[-1]
    count = refs[0].shape[0]
    for place, part in enumerate(refs[:-1]):
        out[count * place : count * (place + 1)] = part[...]


def join_call(*parts):
    shape = (len(parts) * parts[0].shape[0],) + parts[0].shape[1:]
    return pl.pallas_call(
        join_body,
        grid=(1,),
        in_specs=[still(*part.shape) for part in parts],
        out_specs=still(*shape),
        out_shape=jax.ShapeDtypeStruct(shape, BF),
        compiler_params=params(16),
        cost_estimate=cost(0, 100000),
        name="join",
    )(*parts)


def place_body(units, rows, table, *refs):
    groups, parts = refs[:4], refs[-len(units) - (rows > 0) :]
    for index in range(32):
        owner = table[index]
        start = 0
        for part, unit in zip(parts, units):
            part[owner] = groups[index // 8][index % 8, start : start + unit]
            start += unit
    if rows:
        total = jnp.zeros((rows, groups[0].shape[-1]), F32)
        for group in groups:
            for index in range(8):
                total += group[index, start:].astype(F32).reshape(total.shape)
        parts[-1][...] = total


def place_call(table, groups, units, rows=0, after=()):
    width = groups[0].shape[-1]
    shapes = [jax.ShapeDtypeStruct((32, unit, 8, width), BF) for unit in units]
    if rows:
        shapes.append(jax.ShapeDtypeStruct((rows, width), F32))
    return pl.pallas_call(
        functools.partial(place_body, units, rows),
        grid=(1,),
        in_specs=[pl.BlockSpec(memory_space=pltpu.SMEM)]
        + [still(*group.shape) for group in groups]
        + [ANYWHERE] * len(after),
        out_specs=[still(*shape.shape) for shape in shapes],
        out_shape=shapes,
        compiler_params=params(24),
        cost_estimate=cost(0, 4 * 256 * sum(units) * width),
        name="place",
    )(table, *groups, *after)


def gather_flat(count, parts):
    width = parts[0].shape[-1]
    full = lax.all_gather(jnp.concatenate(parts, axis=0), "fsdp", axis=0, tiled=True)
    full = full.reshape(count, -1, width)
    found = []
    start = 0
    for part in parts:
        found.append(full[:, start : start + part.shape[0]].reshape(-1, width))
        start += part.shape[0]
    return found


def together(*arrays):
    return lax.optimization_barrier(arrays)


def fold_body(*refs):
    terms, (keep, send) = refs[:-2], refs[-2:]
    half = keep.shape[0]
    for out, part in ((send, slice(half, 2 * half)), (keep, slice(0, half))):
        total = terms[0][part].astype(F32)
        for term in terms[1:]:
            total += term[part].astype(F32)
        out[...] = total.astype(out.dtype)


def fold_call(*terms):
    shape = (terms[0].shape[0] // 2,) + terms[0].shape[1:]
    return pl.pallas_call(
        fold_body,
        grid=(1,),
        in_specs=[still(*term.shape) for term in terms],
        out_specs=[still(*shape)] * 2,
        out_shape=[jax.ShapeDtypeStruct(shape, F32), jax.ShapeDtypeStruct(shape, BF)],
        compiler_params=params(24),
        cost_estimate=cost(0, 100000),
        name="fold",
    )(*terms)


class Scatter:
    def __init__(self, groups):
        self.groups = groups
        self.came = [swap(groups[3], -1), swap(groups[2], -1)]

    def load(self, step):
        if step == 3:
            send = (self.groups[1].astype(F32) + self.came[0].astype(F32)).astype(BF)
            self.terms = [self.groups[0], self.came[1]]
        else:
            keep, send = fold_call(*self.terms)
            self.terms = [keep]
        return send

    def take(self, step, moved):
        self.terms = self.terms + [moved]

    def result(self):
        total = sum(term.astype(F32) for term in self.terms)
        return total.reshape(-1, total.shape[-1])


def scatter_flat(parts):
    return [lax.psum_scatter(part.astype(F32), "fsdp", scatter_dimension=0, tiled=True) for part in parts]


def shards(
    count,
    tokens,
    cotangent,
    lengths,
    ln1_gain,
    ln1_bias,
    qkv_weight,
    q_bias,
    v_bias,
    out_weight,
    out_bias,
    ln2_gain,
    ln2_bias,
    up_weight,
    up_bias,
    down_weight,
    down_bias,
):
    images, slots, width = tokens.shape
    hops = count == 32
    padded = -(-slots // 16) * 16
    own = width // count
    units = up_bias.shape[0] // CHUNKS
    table = block_table() if hops else None

    singles = [ln1_gain, ln1_bias, q_bias, v_bias, out_bias, ln2_gain, ln2_bias, down_bias, up_bias]
    if hops:
        me = lax.axis_index("fsdp").astype(jnp.int32)
        qkv_units, out_units, feed_units = width * 3 // 256, width // 256, [width // 256] * 4
        held = qkv_weight.T.reshape(1, qkv_units, 8, width)
        three = [swap(held, step) for step in (0, 1, -2)]
        lines = jnp.zeros((16, own), BF).at[:12].set(jnp.concatenate(singles).reshape(12, own))
        out_held = ready_call(me[None], out_weight.T, lines)
        out_came = swap(out_held, 0)
        early, late = ready_feed_call(up_weight.T, down_weight, ())
        *three, out_came, early, late = together(*three, out_came, early, late)
        held = join_call(held, *three)
        came = swap(held, 2)
        out_held = join_call(out_held, out_came)
        out_came = swap(out_held, 1)
        early_came = swap(early, 0)
        came, out_came, early_came = together(came, out_came, early_came)
        held = join_call(held, came)
        across = swap(held, -1)
        came = swap(held, 3)
        out_held = join_call(out_held, out_came)
        out_came = swap(out_held, 2)
        early = join_call(early, early_came)
        early_came = swap(early, 1)
        token_rows, cot_rows = pad_call(tokens, cotangent, padded)
        out_came, token_rows, cot_rows = together(out_came, token_rows, cot_rows)
        out_held = join_call(out_held, out_came)
        out_across = swap(out_held, -1)
        out_came = swap(out_held, 3)
        came, out_came, early_came = together(came, out_came, early_came)
        came_across = swap(came, -1)
        out_came_across = swap(out_came, -1)
        early = join_call(early, early_came)
        early_came = swap(early, 2)
        late_came = swap(late, 0)
        out_full, vectors = place_call(
            table, (out_held, out_came, out_across, out_came_across), [out_units], 16
        )
        out_full = out_full.reshape(-1, width)
        qkv_parts = (held, came, across, came_across)
    else:
        down_rows = down_weight.reshape(count, CHUNKS, units, own).transpose(1, 3, 0, 2)
        down_rows = down_rows.reshape(CHUNKS, own, width)
        up_rows = up_weight.T.reshape(CHUNKS, units, width)
        vector = jnp.concatenate(singles)
        extra = jnp.zeros((8, width), BF).at[0, : vector.shape[0]].set(vector)
        qkv_full, extra, out_full = gather_flat(count, [qkv_weight.T, extra, out_weight.T])
        up_full = gather_flat(count, [up_rows[chunk] for chunk in range(CHUNKS)])
        down_full = gather_flat(count, [down_rows[chunk] for chunk in range(CHUNKS)])
        extra = extra.reshape(count, 8, width)[:, 0, : vector.shape[0]].astype(F32)
        vectors = extra.reshape(count, 12, own).transpose(1, 0, 2).reshape(12, width)
        vectors = jnp.pad(vectors, ((0, 4), (0, 0)))
        qkv_parts = (qkv_full,)
        token_rows, cot_rows = pad_call(tokens, cotangent, padded)

    table = table if hops else lengths
    normed_one, qkv, *found = qkv_call(table, token_rows, vectors, qkv_parts)
    if hops:
        (qkv_full,) = found
        qkv, early_came, late_came = together(qkv, early_came, late_came)
        early = join_call(early, early_came)
        early_across = swap(early, -1)
        early_came = swap(early, 3)
        late = join_call(late, late_came)
        late_came = swap(late, 1)
    found = attend_call(lengths, qkv, token_rows, vectors, out_full, 0, 2)
    if hops:
        partly, late_came = together(found[2], late_came)
        found = [found[0], found[1], partly]
        late = join_call(late, late_came)
        late_came = swap(late, 2)
    found = attend_call(lengths, qkv, token_rows, vectors, out_full, 1, 2, found)
    mixture, middle, normed_two = found

    sums = []
    if hops:
        normed_two, early_came, late_came = together(normed_two, early_came, late_came)
        late = join_call(late, late_came)
        early_groups = (early, early_came, early_across, swap(early_came, -1))
        late_across = swap(late, -1)
        late_came = swap(late, 3)
        feed, back, bias_grad, *found = feed_call(
            0, table, normed_two, cot_rows, early_groups, vectors, (), True
        )
        feed, late_came, late_across = together(feed, late_came, late_across)
        first = Scatter(found)
        late_groups = (late, late_came, late_across, swap(late_came, -1))
        *first.came, feed, late_groups = together(*first.came, feed, late_groups)
        load, feed = together(first.load(3), feed)
        moved = swap(load, 3)
        output, grad_middle, grad_low, close_sums, bias_more, *found = feed_call(
            2,
            table,
            normed_two,
            cot_rows,
            late_groups,
            vectors,
            (feed, back),
            True,
            (middle, mixture),
            slots,
        )
        grad_low, moved, *found = together(grad_low, moved, *found)
        first.take(3, moved)
        second = Scatter(found)
        grad_low, *second.came = together(grad_low, *second.came)
        load, load_two, grad_low = together(first.load(2), second.load(3), grad_low)
        moved_two = swap(load_two, 3)
        moved = swap(load, 2)
        (grad_qkv,) = attend_back_call(lengths, qkv, grad_low, out_full, 0, 1)
        grad_qkv, moved, moved_two = together(grad_qkv, moved, moved_two)
        first.take(2, moved)
        second.take(3, moved_two)
        load, load_two, grad_qkv = together(first.load(1), second.load(2), grad_qkv)
        moved_two = swap(load_two, 2)
        moved = swap(load, 1)
        bias_grads = [bias_grad, bias_more]
        last = Scatter(cross_call(table, grad_qkv, normed_one))
        load, grad_qkv = together(last.load(3), grad_qkv)
        moved_last = swap(load, 3)
    else:
        totals, bias_grads = (), []
        for chunk in range(CHUNKS):
            weights = (up_full[chunk], down_full[chunk])
            feed, back, bias_grad, *found = feed_call(
                chunk, table, normed_two, cot_rows, weights, vectors, totals
            )
            totals = (feed, back)
            bias_grads.append(bias_grad)
            sums.append(jnp.concatenate(scatter_flat(found)))
        output, grad_middle, grad_low, close_sums = close_call(
            middle, cot_rows, vectors, feed, back, images, slots
        )
        (out_sum,) = scatter_flat([cross_flat_call(grad_low, mixture)])
        (grad_qkv,) = attend_back_call(lengths, qkv, grad_low, out_full, 0, 1)
        (qkv_sum,) = scatter_flat([cross_flat_call(grad_qkv, normed_one)])
    grad_input, vector_sums = enter_call(
        token_rows, grad_qkv, grad_middle, vectors, qkv_full, close_sums, bias_grads, images, slots
    )
    if hops:
        vector_sums, grad_input, output, moved = together(vector_sums, grad_input, output, moved)
        first.take(1, moved)
        moved = swap(first.load(0), 0)
        vector_sums += swap(vector_sums, -1)
        moved_vec = [swap(vector_sums, step) for step in (0, 1, -2)]
        moved_last, moved_two, *moved_vec = together(moved_last, moved_two, *moved_vec)
        last.take(3, moved_last)
        second.take(2, moved_two)
        load, moved_two, *moved_vec = together(last.load(2), moved_two, *moved_vec)
        moved_last = swap(load, 2)
        moved_two = swap(second.load(1), 1)
        vector_sums += sum(moved_vec)
        moved_vec = swap(vector_sums, 2)
        moved_last, moved_vec, moved, moved_two = together(moved_last, moved_vec, moved, moved_two)
        total = last.terms[0] + moved_last.astype(F32)
        low, moved_vec, moved, moved_two = together(
            total[1:].astype(BF), moved_vec, moved, moved_two
        )
        three = [swap(low[place : place + 1], step) for place, step in enumerate((0, 1, -2))]
        second.take(1, moved_two)
        moved_two = swap(second.load(0), 0)
        vector_sums += moved_vec
        vector_sums += swap(vector_sums, 3)
        first.take(0, moved)
        second.take(0, moved_two)
        for chain in (first, second):
            found = chain.result()
            sums += [found[: 2 * own], found[2 * own : 4 * own]]
        out_sum = found[4 * own :]
    else:
        vector_sums = lax.psum(vector_sums, "fsdp")
    place = lax.axis_index("fsdp") * own
    vector_sums = lax.dynamic_slice(vector_sums, (0, place), (16, own))
    vec = [vector_sums[row] for row in (0, 1, 2, 3, 7, 4, 5, 6)]

    up_sum = jnp.concatenate([found[:units] for found in sums]).T
    down_sum = jnp.stack([found[units:] for found in sums]).reshape(CHUNKS, own, count, units)
    down_sum = down_sum.transpose(2, 0, 3, 1).reshape(count * CHUNKS * units, own)
    if hops:
        *three, up_sum, down_sum = together(*three, up_sum, down_sum)
        last.terms = [total[:1], *three]
        qkv_sum = last.result()
    return (
        output,
        grad_input,
        vec[0],
        vec[1],
        qkv_sum.T,
        vec[2],
        vec[3],
        out_sum.T,
        vec[4],
        vec[5],
        vec[6],
        up_sum,
        vector_sums[8:12].reshape(-1),
        down_sum,
        vec[7],
    )


def solution(mesh):
    row, column, vector = P("fsdp", None, None), P(None, "fsdp"), P("fsdp")
    return jax.shard_map(
        functools.partial(shards, mesh.shape["fsdp"]),
        mesh=mesh,
        in_specs=(row, row, vector, vector, vector, column, vector, vector, column, vector)
        + (vector, vector, column, vector, column, vector),
        out_specs=(row, row, vector, vector, column, vector, vector, column, vector)
        + (vector, vector, column, vector, column, vector),
        check_vma=False,
    )
```

```python
import functools

import jax
import jax.numpy as jnp
from jax import lax
from jax.experimental import pallas as pl
from jax.experimental.pallas import tpu as pltpu
from jax.sharding import PartitionSpec as P

H = 12
HD = 64
EPS = 1e-06
BF = jnp.bfloat16
F32 = jnp.float32
MIB = 1024 * 1024
CHUNKS = 4
COST = 8
FEED_MIB = 54


def dot(left, right, left_dim, right_dim):
    return lax.dot_general(
        left, right, (((left_dim,), (right_dim,)), ((), ())), preferred_element_type=F32
    )


def norm_parts(values):
    center = values - jnp.mean(values, axis=-1, keepdims=True)
    rscale = lax.rsqrt(jnp.mean(center * center, axis=-1, keepdims=True) + EPS)
    return center * rscale, rscale


def norm_back(grad_normal, normal, rscale):
    grad_mean = jnp.mean(grad_normal, axis=-1, keepdims=True)
    grad_cross = jnp.mean(grad_normal * normal, axis=-1, keepdims=True)
    return rscale * (grad_normal - grad_mean - normal * grad_cross)


def gelu_parts(values):
    size = jnp.abs(values)
    step = 1.0 / (1.0 + (0.3275911 * 0.7071067811865476) * size)
    bell = jnp.exp(-0.5 * values * values)
    poly = 1.061405429 * 0.5
    for factor in (-1.453152027, 1.421413741, -0.284496736, 0.254829592):
        poly = poly * step + 0.5 * factor
    tail = poly * step * bell
    return jnp.where(values >= 0, 1.0 - tail, tail), values * bell * 0.3989422804014327


def params(mib=24):
    return pltpu.CompilerParams(vmem_limit_bytes=mib * MIB)


def waiting(body, inputs, spare):
    return lambda *refs: body(*refs[:inputs], *refs[inputs + spare :])


ANYWHERE = pl.BlockSpec(memory_space=pl.ANY)


def cost(flops, moved):
    return pl.CostEstimate(flops=flops // COST, bytes_accessed=moved // COST, transcendentals=0)


def still(*shape):
    return pl.BlockSpec(shape, lambda *_: (0,) * len(shape), pipeline_mode=pl.Buffered(1))


def qkv_body(kinds, table, tokens, vectors, *refs):
    weights, refs = refs[:kinds], refs[kinds:]
    normed, qkv = refs[:2]
    step = pl.program_id(0)
    width = tokens.shape[1]

    @pl.when(step == 0)
    def first():
        if kinds > 1:
            full, held = refs[2:]
            for index in range(32):
                held[table[index]] = weights[index // 8][index % 8]
            full[...] = held[...].reshape(full.shape)
        rows = normed.shape[0] // 13

        def block(index, carry):
            at = pl.ds(pl.multiple_of(index * rows, rows), rows)
            normal, _ = norm_parts(tokens[at, :].astype(F32))
            normed[at, :] = (normal * vectors[0:1, :] + vectors[1:2, :]).astype(BF)
            return carry

        lax.fori_loop(0, 13, block, 0)

    full = refs[2] if kinds > 1 else weights[0]
    weight = full[pl.ds(pl.multiple_of(step * width, width), width), :]
    zero = jnp.zeros_like(vectors[2:3, :])
    bias = jnp.where(step == 0, vectors[2:3, :], jnp.where(step == 2, vectors[3:4, :], zero))
    qkv[...] = (dot(normed[...], weight, 1, 1) + bias).astype(BF)


def qkv_call(table, tokens, vectors, weights):
    rows, width = tokens.shape
    grouped = len(weights) > 1
    specs = [pl.BlockSpec((rows, width), lambda j: (0, 0)), pl.BlockSpec((rows, width), lambda j: (0, j))]
    shapes = [jax.ShapeDtypeStruct((rows, width), BF), jax.ShapeDtypeStruct((rows, 3 * width), BF)]
    if grouped:
        specs.append(still(3 * width, width))
        shapes.append(jax.ShapeDtypeStruct((3 * width, width), BF))
    return pl.pallas_call(
        functools.partial(qkv_body, len(weights)),
        grid=(3,),
        in_specs=[pl.BlockSpec(memory_space=pltpu.SMEM), still(rows, width), still(16, width)]
        + [still(*array.shape) for array in weights],
        out_specs=specs,
        out_shape=shapes,
        scratch_shapes=[pltpu.VMEM((32, 3 * width // 256, 8, width), BF)] if grouped else [],
        compiler_params=params(),
        cost_estimate=cost(6 * rows * width * width, 2 * (5 * rows * width + 3 * width * width)),
        name="qkv",
    )(table, tokens, vectors, *weights)


def attend_body(first, lengths, qkv, tokens, vectors, weight, _, mixture, middle, normed):
    slots, width = tokens.shape
    live = lax.broadcasted_iota(jnp.int32, (slots, slots), 1) < lengths[pl.program_id(0) + first]
    near = lax.broadcasted_iota(jnp.int32, (slots, 2 * HD), 1) < HD
    for pair in range(H // 2):
        at = 2 * HD * pair
        query = qkv[:, at : at + 2 * HD] * HD**-0.5
        key = qkv[:, width + at : width + at + 2 * HD]
        value = qkv[:, 2 * width + at : 2 * width + at + 2 * HD]
        mixed = []
        for half in (near, ~near):
            scores = dot(jnp.where(half, query, 0), key, 1, 1)
            scores = jnp.where(live, scores, -1e30)
            powers = jnp.exp(scores - jnp.max(scores, axis=1, keepdims=True))
            weights = powers * (1.0 / jnp.sum(powers, axis=1, keepdims=True))
            mixed.append(dot(weights.astype(BF), value, 1, 0))
        mixture[:, at : at + 2 * HD] = jnp.where(near, mixed[0], mixed[1]).astype(BF)
    branch = dot(mixture[...], weight[...], 1, 1)
    middle[...] = branch + (tokens[...].astype(F32) + vectors[4:5, :])
    normal, _ = norm_parts(middle[...])
    normed[...] = (normal * vectors[5:6, :] + vectors[6:7, :]).astype(BF)


def attend_call(lengths, qkv, tokens, vectors, weight, part, parts, earlier=(), after=()):
    rows, width = tokens.shape
    images = lengths.shape[0]
    slots = rows // images
    first = part * images // parts
    spare = list(earlier) + list(after)
    row = pl.BlockSpec((slots, width), lambda i, *_: (i + first, 0))
    return pl.pallas_call(
        waiting(functools.partial(attend_body, first), 6, len(spare)),
        grid_spec=pltpu.PrefetchScalarGridSpec(
            num_scalar_prefetch=1,
            grid=(images // parts,),
            in_specs=[
                pl.BlockSpec((slots, 3 * width), lambda i, *_: (i + first, 0)),
                row,
                still(16, width),
                still(width, width),
            ]
            + [ANYWHERE] * (len(spare) + 1),
            out_specs=[row, row, row],
        ),
        out_shape=[
            jax.ShapeDtypeStruct((rows, width), BF),
            jax.ShapeDtypeStruct((rows, width), F32),
            jax.ShapeDtypeStruct((rows, width), BF),
        ],
        input_output_aliases={6 + place: place for place in range(len(earlier))},
        compiler_params=params(),
        cost_estimate=cost(16 * rows * width * width // parts, 16 * rows * width // parts),
        name="attend",
    )(lengths, qkv, tokens, vectors, weight, lengths, *spare)


def close_rows(values, total, behind, given, vectors):
    normal, rscale = norm_parts(values)
    grad = given + norm_back(behind * vectors[5:6, :], normal, rscale)
    low = grad.astype(BF)
    return values + total + vectors[7:8, :], grad, low, (behind * normal, behind, given, low.astype(F32))


def feed_body(hops, begin, chunk, table, normed, cot, bias, *refs):
    tiles = 2 if hops else 1
    close = hops and not begin
    weights, refs = refs[: 2 * tiles], refs[2 * tiles :]
    if not begin:
        feed_in, back_in, refs = refs[0], refs[1], refs[2:]
    if close:
        middle, mixture, output, grad_middle, grad_low, sums, *refs = refs
        sums[...] = jnp.zeros_like(sums)
    else:
        feed, back, *refs = refs
    bias_grad, *refs = refs
    hidden, slope = refs[-2:]
    slots = normed.shape[0] // 4
    width = normed.shape[1]
    if hops:
        groups, held, flat = refs[:4], refs[4], refs[5]
        units = weights[0].shape[1] // 4
        for index in range(32):
            held[table[index], : 4 * units] = weights[index // 8][index % 8]
        for place in range(4):
            flat[place] = held[:, units * place : units * (place + 1)].reshape(width, width)
    for part in range(4):
        at = slice(slots * part, slots * (part + 1))
        ahead = 0.0 if begin else feed_in[at, :]
        behind = 0.0 if begin else back_in[at, :]
        for tile in range(tiles):
            up = flat[2 * tile] if hops else weights[0][...]
            down = flat[2 * tile + 1] if hops else weights[1][...]
            row = 8 + chunk + tile
            before = dot(normed[at, :], up, 1, 1) + bias[row : row + 1, :]
            grad = dot(cot[at, :], down, 1, 0)
            share, bend = gelu_parts(before)
            hidden[tile, at, :] = (before * share).astype(BF)
            low = (grad * (share + bend)).astype(BF)
            slope[tile, at, :] = low
            total = jnp.sum(low.astype(F32), axis=0, keepdims=True)
            if part == 0:
                bias_grad[tile : tile + 1, :] = total
            else:
                bias_grad[tile : tile + 1, :] += total
            ahead += dot(hidden[tile, at, :], down, 1, 1)
            behind += dot(low, up, 1, 0)
        if not close:
            feed[at, :] = ahead
            back[at, :] = behind
            continue
        result, grad, low, terms = close_rows(
            middle[at, :], ahead, behind, cot[at, :].astype(F32), bias
        )
        output[part] = result[: output.shape[1]].astype(BF)
        grad_middle[at, :] = grad
        grad_low[at, :] = low
        for place, term in enumerate(terms):
            sums[place : place + 1, :] += jnp.sum(term, axis=0, keepdims=True)
    if close:
        found = dot(grad_low[...], mixture[...], 0, 0)
        for owner in range(32):
            block = found[8 * units * owner : 8 * units * (owner + 1)]
            held[owner, 4 * units :] = eights(block).astype(BF)
    for tile in range(tiles):
        found = [dot(slope[tile], normed[...], 0, 0), dot(cot[...], hidden[tile], 0, 0)]
        if not hops:
            refs[0][...] = found[0].astype(BF)
            refs[1][...] = found[1].astype(BF)
            return
        for owner in range(32):
            for place in range(2):
                block = found[place][8 * units * owner : 8 * units * (owner + 1)]
                spot = units * (2 * tile + place)
                held[owner, spot : spot + units] = eights(block).astype(BF)
    deal(table, held, groups)


def feed_call(chunk, table, normed, cot, weights, vectors, sums=(), hops=False, ends=(), slots=0):
    rows, width = normed.shape
    tiles = 2 if hops else 1
    total = jax.ShapeDtypeStruct((rows, width), F32)
    if ends:
        shapes = [
            jax.ShapeDtypeStruct((4, slots, width), BF),
            total,
            jax.ShapeDtypeStruct((rows, width), BF),
            jax.ShapeDtypeStruct((8, width), F32),
        ]
    else:
        shapes = [total, total]
    shapes.append(jax.ShapeDtypeStruct((tiles, width), F32))
    scratch = [pltpu.VMEM((tiles, rows, width), BF)] * 2
    if hops:
        units = (5 if ends else 4) * width // 256
        shapes += group_shapes(units, width)
        held = [pltpu.VMEM((32, units, 8, width), BF), pltpu.VMEM((4, width, width), BF)]
        scratch = held + scratch
    else:
        shapes += [jax.ShapeDtypeStruct((width, width), BF)] * 2
    arrays = [normed, cot, vectors, *weights, *sums, *ends]
    return pl.pallas_call(
        functools.partial(feed_body, hops, not sums, chunk),
        grid=(1,),
        in_specs=[pl.BlockSpec(memory_space=pltpu.SMEM)] + [still(*array.shape) for array in arrays],
        out_specs=[still(*shape.shape) for shape in shapes],
        out_shape=shapes,
        scratch_shapes=scratch,
        compiler_params=params(FEED_MIB),
        cost_estimate=cost(12 * tiles * rows * width * width, 20 * rows * width),
        name="feed",
    )(table, *arrays)


def close_body(middle, cot, vectors, feed, back, output, grad_middle, grad_low, sums):
    result, grad, low, terms = close_rows(
        middle[...], feed[...], back[...], cot[...].astype(F32), vectors
    )
    output[0] = result[: output.shape[1]].astype(BF)
    grad_middle[...] = grad
    grad_low[...] = low

    @pl.when(pl.program_id(0) == 0)
    def start():
        sums[...] = jnp.zeros_like(sums)

    for place, term in enumerate(terms):
        sums[place : place + 1, :] += jnp.sum(term, axis=0, keepdims=True)


def close_call(middle, cot, vectors, feed, back, images, slots, after=()):
    rows, width = middle.shape
    row = pl.BlockSpec((rows // images, width), lambda i: (i, 0))
    fixed = pl.BlockSpec((8, width), lambda i: (0, 0))
    steady = still(16, width)
    return pl.pallas_call(
        waiting(close_body, 5, len(after)),
        grid=(images,),
        in_specs=[row, row, steady, row, row] + [ANYWHERE] * len(after),
        out_specs=[pl.BlockSpec((1, slots, width), lambda i: (i, 0, 0)), row, row, fixed],
        out_shape=[
            jax.ShapeDtypeStruct((images, slots, width), BF),
            jax.ShapeDtypeStruct((rows, width), F32),
            jax.ShapeDtypeStruct((rows, width), BF),
            jax.ShapeDtypeStruct((8, width), F32),
        ],
        compiler_params=params(),
        cost_estimate=cost(5000 * rows * width, 30 * rows * width),
        name="close",
    )(middle, cot, vectors, feed, back, *after)


def attend_back_body(first, lengths, qkv, grad_low, weight, _, grad_qkv, grad_mix):
    slots, width = grad_low.shape
    live = lax.broadcasted_iota(jnp.int32, (slots, slots), 0) < lengths[pl.program_id(0) + first]
    near = lax.broadcasted_iota(jnp.int32, (slots, 2 * HD), 1) < HD
    grad_mix[...] = dot(grad_low[...], weight[...], 1, 0).astype(BF)
    for pair in range(H // 2):
        at = 2 * HD * pair
        query = qkv[:, at : at + 2 * HD] * HD**-0.5
        key = qkv[:, width + at : width + at + 2 * HD]
        value = qkv[:, 2 * width + at : 2 * width + at + 2 * HD]
        mix = grad_mix[:, at : at + 2 * HD]
        found = []
        for half in (near, ~near):
            scores = dot(key, jnp.where(half, query, 0), 1, 1)
            scores = jnp.where(live, scores, -1e30)
            powers = jnp.exp(scores - jnp.max(scores, axis=0, keepdims=True))
            weights = powers * (1.0 / jnp.sum(powers, axis=0, keepdims=True))
            slope = dot(value, jnp.where(half, mix, 0), 1, 1)
            grad_value = dot(weights.astype(BF), mix, 1, 0)
            inner = jnp.sum(slope * weights, axis=0, keepdims=True)
            low = (weights * (slope - inner)).astype(BF)
            grad_key = dot(low, query, 1, 0)
            grad_query = dot(low, key * HD**-0.5, 0, 0)
            found.append((grad_query, grad_key, grad_value))
        for place in range(3):
            grad_qkv[:, place * width + at : place * width + at + 2 * HD] = jnp.where(
                near, found[0][place], found[1][place]
            ).astype(BF)


def attend_back_call(lengths, qkv, grad_low, weight, part, parts, earlier=(), after=()):
    rows, width = grad_low.shape
    images = lengths.shape[0]
    slots = rows // images
    first = part * images // parts
    spare = list(earlier) + list(after)
    wide = pl.BlockSpec((slots, 3 * width), lambda i, *_: (i + first, 0))
    return pl.pallas_call(
        waiting(functools.partial(attend_back_body, first), 5, len(spare)),
        grid_spec=pltpu.PrefetchScalarGridSpec(
            num_scalar_prefetch=1,
            grid=(images // parts,),
            in_specs=[
                wide,
                pl.BlockSpec((slots, width), lambda i, *_: (i + first, 0)),
                still(width, width),
            ]
            + [ANYWHERE] * (1 + len(spare)),
            out_specs=[wide],
            scratch_shapes=[pltpu.VMEM((slots, width), BF)],
        ),
        out_shape=[jax.ShapeDtypeStruct((rows, 3 * width), BF)],
        input_output_aliases={5: 0} if earlier else {},
        compiler_params=params(),
        cost_estimate=cost(30 * rows * width * width // parts, 16 * rows * width // parts),
        name="attend_back",
    )(lengths, qkv, grad_low, weight, lengths, *spare)


def cross_flat_body(left, right, out):
    out[...] = dot(left[...], right[...], 0, 0).astype(BF)


def cross_flat_call(left, right):
    rows, width = right.shape
    wide = left.shape[1]
    return pl.pallas_call(
        cross_flat_body,
        grid=(wide // width,),
        in_specs=[
            pl.BlockSpec((rows, width), lambda j: (0, j)),
            pl.BlockSpec((rows, width), lambda j: (0, 0)),
        ],
        out_specs=pl.BlockSpec((width, width), lambda j: (j, 0)),
        out_shape=jax.ShapeDtypeStruct((wide, width), BF),
        compiler_params=params(),
        cost_estimate=cost(2 * rows * width * wide, 2 * rows * (width + wide) + 2 * wide * width),
        name="cross",
    )(left, right)


def deal(table, held, groups):
    for index in range(32):
        groups[index // 8][index % 8] = held[table[index]]


def group_shapes(units, width):
    return [jax.ShapeDtypeStruct((8, units, 8, width), BF)] * 4


def cross_body(spare, table, left, right, *refs):
    refs = refs[spare:]
    groups, whole, held = refs[:4], refs[4], refs[5]
    step = pl.program_id(0)
    steps = pl.num_programs(0)
    width = right.shape[1]
    for index in range(whole.shape[0] // width):
        @pl.when(step == index)
        def tile():
            whole[width * index : width * (index + 1), :] = dot(left[...], right[...], 0, 0)

    @pl.when(step == steps - 1)
    def last():
        units = held.shape[1]
        for owner in range(32):
            block = whole[8 * units * owner : 8 * units * (owner + 1), :]
            held[owner] = block.reshape(units, 8, width).astype(BF)
        deal(table, held, groups)


def cross_call(table, left, right, after=()):
    rows, width = right.shape
    wide = left.shape[1]
    units = wide // 256
    group = pl.BlockSpec((8, units, 8, width), lambda j, *_: (0, 0, 0, 0))
    return pl.pallas_call(
        functools.partial(cross_body, len(after)),
        grid_spec=pltpu.PrefetchScalarGridSpec(
            num_scalar_prefetch=1,
            grid=(wide // width,),
            in_specs=[
                pl.BlockSpec((rows, width), lambda j, *_: (0, j)),
                pl.BlockSpec((rows, width), lambda j, *_: (0, 0)),
            ]
            + [ANYWHERE] * len(after),
            out_specs=[group] * 4,
            scratch_shapes=[pltpu.VMEM((wide, width), F32), pltpu.VMEM((32, units, 8, width), BF)],
        ),
        out_shape=group_shapes(units, width),
        compiler_params=params(),
        cost_estimate=cost(2 * rows * width * wide, 2 * rows * (width + wide) + 2 * wide * width),
        name="cross",
    )(table, left, right, *after)


def enter_body(tokens, grad_qkv, grad_middle, vectors, weight, close_sums, *refs):
    biases, (grad_input, sums) = refs[:-2], refs[-2:]
    slots, width = grad_input.shape[1:]
    low = grad_qkv[...]
    grad = dot(low, weight[...], 1, 0)
    normal, rscale = norm_parts(tokens[...].astype(F32))
    full = grad_middle[...] + norm_back(grad * vectors[0:1, :], normal, rscale)
    grad_input[0] = full[:slots]

    @pl.when(pl.program_id(0) == 0)
    def start():
        sums[...] = jnp.zeros_like(sums)
        sums[4:8, :] = close_sums[0:4, :]
        each = biases[0].shape[0]
        for place, bias in enumerate(biases):
            sums[8 + each * place : 8 + each * (place + 1), :] = bias[...]

    query_value = [low[:, :width], low[:, 2 * width :]]
    for place, term in enumerate([grad * normal, grad] + query_value):
        sums[place : place + 1, :] += jnp.sum(term.astype(F32), axis=0, keepdims=True)


def enter_call(tokens, grad_qkv, grad_middle, vectors, weight, close_sums, biases, images, slots):
    rows, width = tokens.shape
    row = pl.BlockSpec((rows // images, width), lambda i: (i, 0))
    return pl.pallas_call(
        enter_body,
        grid=(images,),
        in_specs=[
            row,
            pl.BlockSpec((rows // images, 3 * width), lambda i: (i, 0)),
            row,
            still(16, width),
            still(3 * width, width),
            still(8, width),
        ]
        + [still(*bias.shape) for bias in biases],
        out_specs=[
            pl.BlockSpec((1, slots, width), lambda i: (i, 0, 0)),
            pl.BlockSpec((16, width), lambda i: (0, 0)),
        ],
        out_shape=[
            jax.ShapeDtypeStruct((images, slots, width), F32),
            jax.ShapeDtypeStruct((16, width), F32),
        ],
        compiler_params=params(),
        cost_estimate=cost(6 * rows * width * width, 20 * rows * width),
        name="enter",
    )(tokens, grad_qkv, grad_middle, vectors, weight, close_sums, *biases)


ORDERS = ((8, 16, 2, 4), (16, 8, 4, 2))


def reach(order):
    return [sum(order[bit] for bit in range(4) if index >> bit & 1) for index in range(16)]


def block_table():
    me = lax.axis_index("fsdp")
    near, far = reach(ORDERS[0]), reach(ORDERS[1])
    even = jnp.array(near + [1 ^ place for place in far], jnp.int32)
    odd = jnp.array(far + [1 ^ place for place in near], jnp.int32)
    return jnp.bitwise_xor(jnp.where(me % 2 == 0, even, odd), me.astype(jnp.int32))


def swap(values, step):
    pairs = []
    for index in range(32):
        order = ORDERS[index % 2]
        flip = 1 if step == -1 else order[0] ^ order[1] if step == -2 else order[step]
        pairs.append((index, index ^ flip))
    return lax.ppermute(values, "fsdp", pairs)


def turned(values):
    size = values.shape[1]
    unit = lax.broadcasted_iota(jnp.int32, (size, size), 0) == lax.broadcasted_iota(
        jnp.int32, (size, size), 1
    )
    return dot(unit.astype(BF), values, 1, 1)


def eights(values):
    return values.reshape(values.shape[0] // 8, 8, values.shape[1])


def ready_body(me, rows, lines, out):
    own, width = lines.shape[1], out.shape[3]
    units = rows.shape[0] // 8
    out[0, :units] = eights(rows[...])
    places = lax.broadcasted_iota(jnp.int32, (own, width), 0) + me[0] * own
    spread = (places == lax.broadcasted_iota(jnp.int32, (own, width), 1)).astype(BF)
    out[0, units:] = eights(dot(lines[...], spread, 1, 0)).astype(BF)


def ready_call(me, rows, lines):
    width = rows.shape[1]
    shape = (1, (rows.shape[0] + lines.shape[0]) // 8, 8, width)
    return pl.pallas_call(
        ready_body,
        grid=(1,),
        in_specs=[pl.BlockSpec(memory_space=pltpu.SMEM), still(*rows.shape), still(*lines.shape)],
        out_specs=still(*shape),
        out_shape=jax.ShapeDtypeStruct(shape, BF),
        compiler_params=params(8),
        cost_estimate=cost(0, 1000000),
        name="ready",
    )(me, rows, lines)


def ready_feed_body(up, down, *refs):
    early, late = refs[-2:]
    many = up.shape[0] // CHUNKS
    count = down.shape[0] // (CHUNKS * many)
    own = down.shape[1]
    split = down[...].astype(F32).reshape(count, CHUNKS, many, own)
    for chunk in range(CHUNKS):
        held = turned(split[:, chunk].reshape(count * many, own).astype(BF))
        both = [eights(up[many * chunk : many * (chunk + 1), :].astype(F32)), eights(held)]
        out = early if chunk < CHUNKS // 2 else late
        start = chunk % (CHUNKS // 2) * (many + own) // 8
        out[0, start : start + many // 8] = both[0].astype(BF)
        out[0, start + many // 8 : start + (many + own) // 8] = both[1].astype(BF)


def ready_feed_call(up, down, after):
    width = up.shape[1]
    shape = (1, (up.shape[0] + down.shape[1] * CHUNKS) // 16, 8, width)
    return pl.pallas_call(
        ready_feed_body,
        grid=(1,),
        in_specs=[still(*up.shape), still(*down.shape)] + [ANYWHERE] * len(after),
        out_specs=[still(*shape)] * 2,
        out_shape=[jax.ShapeDtypeStruct(shape, BF)] * 2,
        compiler_params=params(16),
        cost_estimate=cost(0, 1000000),
        name="ready_feed",
    )(up, down, *after)


def pad_body(tokens, cot, *refs):
    for given, out in zip((tokens, cot), refs[-2:]):
        slots = given.shape[1]
        out[...] = jnp.zeros_like(out)
        out[:slots, :] = given[0]


def pad_call(tokens, cot, padded, after=()):
    images, slots, width = tokens.shape
    block = pl.BlockSpec((1, slots, width), lambda i: (i, 0, 0))
    row = pl.BlockSpec((padded, width), lambda i: (i, 0))
    return pl.pallas_call(
        pad_body,
        grid=(images,),
        in_specs=[block, block] + [ANYWHERE] * len(after),
        out_specs=[row, row],
        out_shape=[jax.ShapeDtypeStruct((images * padded, width), BF)] * 2,
        compiler_params=params(16),
        cost_estimate=cost(0, 1000000),
        name="pad",
    )(tokens, cot, *after)


def join_body(*refs):
    out = refs[-1]
    count = refs[0].shape[0]
    for place, part in enumerate(refs[:-1]):
        out[count * place : count * (place + 1)] = part[...]


def join_call(*parts):
    shape = (len(parts) * parts[0].shape[0],) + parts[0].shape[1:]
    return pl.pallas_call(
        join_body,
        grid=(1,),
        in_specs=[still(*part.shape) for part in parts],
        out_specs=still(*shape),
        out_shape=jax.ShapeDtypeStruct(shape, BF),
        compiler_params=params(16),
        cost_estimate=cost(0, 100000),
        name="join",
    )(*parts)


def place_body(units, rows, table, *refs):
    groups, parts = refs[:4], refs[-len(units) - (rows > 0) :]
    for index in range(32):
        owner = table[index]
        start = 0
        for part, unit in zip(parts, units):
            part[owner] = groups[index // 8][index % 8, start : start + unit]
            start += unit
    if rows:
        total = jnp.zeros((rows, groups[0].shape[-1]), F32)
        for group in groups:
            for index in range(8):
                total += group[index, start:].astype(F32).reshape(total.shape)
        parts[-1][...] = total


def place_call(table, groups, units, rows=0, after=()):
    width = groups[0].shape[-1]
    shapes = [jax.ShapeDtypeStruct((32, unit, 8, width), BF) for unit in units]
    if rows:
        shapes.append(jax.ShapeDtypeStruct((rows, width), F32))
    return pl.pallas_call(
        functools.partial(place_body, units, rows),
        grid=(1,),
        in_specs=[pl.BlockSpec(memory_space=pltpu.SMEM)]
        + [still(*group.shape) for group in groups]
        + [ANYWHERE] * len(after),
        out_specs=[still(*shape.shape) for shape in shapes],
        out_shape=shapes,
        compiler_params=params(24),
        cost_estimate=cost(0, 4 * 256 * sum(units) * width),
        name="place",
    )(table, *groups, *after)


def gather_flat(count, parts):
    width = parts[0].shape[-1]
    full = lax.all_gather(jnp.concatenate(parts, axis=0), "fsdp", axis=0, tiled=True)
    full = full.reshape(count, -1, width)
    found = []
    start = 0
    for part in parts:
        found.append(full[:, start : start + part.shape[0]].reshape(-1, width))
        start += part.shape[0]
    return found


def together(*arrays):
    return lax.optimization_barrier(arrays)


def fold_body(*refs):
    terms, (keep, send) = refs[:-2], refs[-2:]
    half = keep.shape[0]
    for out, part in ((send, slice(half, 2 * half)), (keep, slice(0, half))):
        total = terms[0][part].astype(F32)
        for term in terms[1:]:
            total += term[part].astype(F32)
        out[...] = total.astype(out.dtype)


def fold_call(*terms):
    shape = (terms[0].shape[0] // 2,) + terms[0].shape[1:]
    return pl.pallas_call(
        fold_body,
        grid=(1,),
        in_specs=[still(*term.shape) for term in terms],
        out_specs=[still(*shape)] * 2,
        out_shape=[jax.ShapeDtypeStruct(shape, F32), jax.ShapeDtypeStruct(shape, BF)],
        compiler_params=params(24),
        cost_estimate=cost(0, 100000),
        name="fold",
    )(*terms)


class Scatter:
    def __init__(self, groups):
        self.groups = groups
        self.came = [swap(groups[3], -1), swap(groups[2], -1)]

    def load(self, step):
        if step == 3:
            send = (self.groups[1].astype(F32) + self.came[0].astype(F32)).astype(BF)
            self.terms = [self.groups[0], self.came[1]]
        else:
            keep, send = fold_call(*self.terms)
            self.terms = [keep]
        return send

    def take(self, step, moved):
        self.terms = self.terms + [moved]

    def result(self):
        total = sum(term.astype(F32) for term in self.terms)
        return total.reshape(-1, total.shape[-1])


def scatter_flat(parts):
    return [lax.psum_scatter(part.astype(F32), "fsdp", scatter_dimension=0, tiled=True) for part in parts]


def shards(
    count,
    tokens,
    cotangent,
    lengths,
    ln1_gain,
    ln1_bias,
    qkv_weight,
    q_bias,
    v_bias,
    out_weight,
    out_bias,
    ln2_gain,
    ln2_bias,
    up_weight,
    up_bias,
    down_weight,
    down_bias,
):
    images, slots, width = tokens.shape
    hops = count == 32
    padded = -(-slots // 16) * 16
    own = width // count
    units = up_bias.shape[0] // CHUNKS
    table = block_table() if hops else None

    singles = [ln1_gain, ln1_bias, q_bias, v_bias, out_bias, ln2_gain, ln2_bias, down_bias, up_bias]
    if hops:
        me = lax.axis_index("fsdp").astype(jnp.int32)
        qkv_units, out_units, feed_units = width * 3 // 256, width // 256, [width // 256] * 4
        held = qkv_weight.T.reshape(1, qkv_units, 8, width)
        three = [swap(held, step) for step in (0, 1, -2)]
        lines = jnp.zeros((16, own), BF).at[:12].set(jnp.concatenate(singles).reshape(12, own))
        out_held = ready_call(me[None], out_weight.T, lines)
        out_came = swap(out_held, 0)
        early, late = ready_feed_call(up_weight.T, down_weight, ())
        *three, out_came, early, late = together(*three, out_came, early, late)
        held = join_call(held, *three)
        came = swap(held, 2)
        out_held = join_call(out_held, out_came)
        out_came = swap(out_held, 1)
        early_came = swap(early, 0)
        came, out_came, early_came = together(came, out_came, early_came)
        held = join_call(held, came)
        across = swap(held, -1)
        came = swap(held, 3)
        out_held = join_call(out_held, out_came)
        out_came = swap(out_held, 2)
        early = join_call(early, early_came)
        early_came = swap(early, 1)
        token_rows, cot_rows = pad_call(tokens, cotangent, padded)
        out_came, token_rows, cot_rows = together(out_came, token_rows, cot_rows)
        out_held = join_call(out_held, out_came)
        out_across = swap(out_held, -1)
        out_came = swap(out_held, 3)
        came, out_came, early_came = together(came, out_came, early_came)
        came_across = swap(came, -1)
        out_came_across = swap(out_came, -1)
        early = join_call(early, early_came)
        early_came = swap(early, 2)
        late_came = swap(late, 0)
        out_full, vectors = place_call(
            table, (out_held, out_came, out_across, out_came_across), [out_units], 16
        )
        out_full = out_full.reshape(-1, width)
        qkv_parts = (held, came, across, came_across)
    else:
        down_rows = down_weight.reshape(count, CHUNKS, units, own).transpose(1, 3, 0, 2)
        down_rows = down_rows.reshape(CHUNKS, own, width)
        up_rows = up_weight.T.reshape(CHUNKS, units, width)
        vector = jnp.concatenate(singles)
        extra = jnp.zeros((8, width), BF).at[0, : vector.shape[0]].set(vector)
        qkv_full, extra, out_full = gather_flat(count, [qkv_weight.T, extra, out_weight.T])
        up_full = gather_flat(count, [up_rows[chunk] for chunk in range(CHUNKS)])
        down_full = gather_flat(count, [down_rows[chunk] for chunk in range(CHUNKS)])
        extra = extra.reshape(count, 8, width)[:, 0, : vector.shape[0]].astype(F32)
        vectors = extra.reshape(count, 12, own).transpose(1, 0, 2).reshape(12, width)
        vectors = jnp.pad(vectors, ((0, 4), (0, 0)))
        qkv_parts = (qkv_full,)
        token_rows, cot_rows = pad_call(tokens, cotangent, padded)

    table = table if hops else lengths
    normed_one, qkv, *found = qkv_call(table, token_rows, vectors, qkv_parts)
    if hops:
        (qkv_full,) = found
        qkv, early_came, late_came = together(qkv, early_came, late_came)
        early = join_call(early, early_came)
        early_across = swap(early, -1)
        early_came = swap(early, 3)
        late = join_call(late, late_came)
        late_came = swap(late, 1)
    found = attend_call(lengths, qkv, token_rows, vectors, out_full, 0, 2)
    if hops:
        partly, late_came = together(found[2], late_came)
        found = [found[0], found[1], partly]
        late = join_call(late, late_came)
        late_came = swap(late, 2)
    found = attend_call(lengths, qkv, token_rows, vectors, out_full, 1, 2, found)
    mixture, middle, normed_two = found

    sums = []
    if hops:
        normed_two, early_came, late_came = together(normed_two, early_came, late_came)
        late = join_call(late, late_came)
        early_groups = (early, early_came, early_across, swap(early_came, -1))
        late_across = swap(late, -1)
        late_came = swap(late, 3)
        feed, back, bias_grad, *found = feed_call(
            0, table, normed_two, cot_rows, early_groups, vectors, (), True
        )
        feed, late_came, late_across = together(feed, late_came, late_across)
        first = Scatter(found)
        late_groups = (late, late_came, late_across, swap(late_came, -1))
        *first.came, feed, late_groups = together(*first.came, feed, late_groups)
        load, feed = together(first.load(3), feed)
        moved = swap(load, 3)
        output, grad_middle, grad_low, close_sums, bias_more, *found = feed_call(
            2,
            table,
            normed_two,
            cot_rows,
            late_groups,
            vectors,
            (feed, back),
            True,
            (middle, mixture),
            slots,
        )
        grad_low, moved, *found = together(grad_low, moved, *found)
        first.take(3, moved)
        second = Scatter(found)
        grad_low, *second.came = together(grad_low, *second.came)
        load, load_two, grad_low = together(first.load(2), second.load(3), grad_low)
        moved_two = swap(load_two, 3)
        moved = swap(load, 2)
        (grad_qkv,) = attend_back_call(lengths, qkv, grad_low, out_full, 0, 1)
        grad_qkv, moved, moved_two = together(grad_qkv, moved, moved_two)
        first.take(2, moved)
        second.take(3, moved_two)
        load, load_two, grad_qkv = together(first.load(1), second.load(2), grad_qkv)
        moved_two = swap(load_two, 2)
        moved = swap(load, 1)
        bias_grads = [bias_grad, bias_more]
        last = Scatter(cross_call(table, grad_qkv, normed_one))
        load, grad_qkv = together(last.load(3), grad_qkv)
        moved_last = swap(load, 3)
    else:
        totals, bias_grads = (), []
        for chunk in range(CHUNKS):
            weights = (up_full[chunk], down_full[chunk])
            feed, back, bias_grad, *found = feed_call(
                chunk, table, normed_two, cot_rows, weights, vectors, totals
            )
            totals = (feed, back)
            bias_grads.append(bias_grad)
            sums.append(jnp.concatenate(scatter_flat(found)))
        output, grad_middle, grad_low, close_sums = close_call(
            middle, cot_rows, vectors, feed, back, images, slots
        )
        (out_sum,) = scatter_flat([cross_flat_call(grad_low, mixture)])
        (grad_qkv,) = attend_back_call(lengths, qkv, grad_low, out_full, 0, 1)
        (qkv_sum,) = scatter_flat([cross_flat_call(grad_qkv, normed_one)])
    grad_input, vector_sums = enter_call(
        token_rows, grad_qkv, grad_middle, vectors, qkv_full, close_sums, bias_grads, images, slots
    )
    if hops:
        vector_sums, grad_input, output, moved = together(vector_sums, grad_input, output, moved)
        first.take(1, moved)
        moved = swap(first.load(0), 0)
        vector_sums += swap(vector_sums, -1)
        moved_vec = [swap(vector_sums, step) for step in (0, 1, -2)]
        moved_last, moved_two, *moved_vec = together(moved_last, moved_two, *moved_vec)
        last.take(3, moved_last)
        second.take(2, moved_two)
        load, moved_two, *moved_vec = together(last.load(2), moved_two, *moved_vec)
        moved_last = swap(load, 2)
        moved_two = swap(second.load(1), 1)
        vector_sums += sum(moved_vec)
        moved_vec = swap(vector_sums, 2)
        moved_last, moved_vec, moved = together(moved_last, moved_vec, moved)
        total = last.terms[0] + moved_last.astype(F32)
        low, moved_vec, moved, moved_two = together(
            total[1:].astype(BF), moved_vec, moved, moved_two
        )
        three = [swap(low[place : place + 1], step) for place, step in enumerate((0, 1, -2))]
        second.take(1, moved_two)
        moved_two = swap(second.load(0), 0)
        vector_sums += moved_vec
        vector_sums += swap(vector_sums, 3)
        first.take(0, moved)
        second.take(0, moved_two)
        for chain in (first, second):
            found = chain.result()
            sums += [found[: 2 * own], found[2 * own : 4 * own]]
        out_sum = found[4 * own :]
    else:
        vector_sums = lax.psum(vector_sums, "fsdp")
    place = lax.axis_index("fsdp") * own
    vector_sums = lax.dynamic_slice(vector_sums, (0, place), (16, own))
    vec = [vector_sums[row] for row in (0, 1, 2, 3, 7, 4, 5, 6)]

    up_sum = jnp.concatenate([found[:units] for found in sums]).T
    down_sum = jnp.stack([found[units:] for found in sums]).reshape(CHUNKS, own, count, units)
    down_sum = down_sum.transpose(2, 0, 3, 1).reshape(count * CHUNKS * units, own)
    if hops:
        *three, up_sum, down_sum = together(*three, up_sum, down_sum)
        last.terms = [total[:1], *three]
        qkv_sum = last.result()
    return (
        output,
        grad_input,
        vec[0],
        vec[1],
        qkv_sum.T,
        vec[2],
        vec[3],
        out_sum.T,
        vec[4],
        vec[5],
        vec[6],
        up_sum,
        vector_sums[8:12].reshape(-1),
        down_sum,
        vec[7],
    )


def solution(mesh):
    row, column, vector = P("fsdp", None, None), P(None, "fsdp"), P("fsdp")
    return jax.shard_map(
        functools.partial(shards, mesh.shape["fsdp"]),
        mesh=mesh,
        in_specs=(row, row, vector, vector, vector, column, vector, vector, column, vector)
        + (vector, vector, column, vector, column, vector),
        out_specs=(row, row, vector, vector, column, vector, vector, column, vector)
        + (vector, vector, column, vector, column, vector),
        check_vma=False,
    )
```
